256 devices in a mesh: imp: 32 (over z, y), camp: 8 (over x, core).
Axes of the slice: x: 4, y: 4, z: 8, core: 2. Of those that a mesh axis runs over, the one named last changes fastest.
Arguments:
- imp_emb: bfloat16 [131072, 256], P(('imp', 'camp')), may hold values from -512 to 512
- imp_cost: bfloat16 [131072], P(('imp', 'camp')), may hold values from 0.099609375 to 1
- camp_emb: bfloat16 [32768, 256], P(('camp', 'imp')), may hold values from -6 to 6
- prices: bfloat16 [32768], P(('camp', 'imp')), may hold values from -5 to 5
- spend_limits: float32 [32768], P(('camp', 'imp')), may hold values from 5 to 64
- block_lists: int32 [1024, 8, 8], P('imp', 'camp'), may hold values from 0 to 31, as said below
- block_counts: int32 [1024, 8], P('imp', 'camp'), may hold values from 1 to 8, as said below
Outputs:
- new_prices: float32 [32768], P(('camp', 'imp'))
- row_logz: float32 [131072], P('imp')
The draws below stay inside these ranges and needn't reach their ends.
Inputs may be any that keep to these rules, and one draw needn't show every extreme that they name: `block_lists`: entries of a list of one tile and owner are distinct block numbers of that owner; slots past the count hold block numbers too, which are ignored. `block_counts`: tile 0 uses all 8 slots of every owner.
All inputs are finite; a program needn't handle non-finite values.
Results may differ from the reference program's by a relative error of at most 0.0003.
Values may be sent and summed in bfloat16 or wider, within the bound.
No kernel may reach another device: no remote copies, remote signals or barrier semaphores. Data moves between devices by JAX's collectives and lax.ppermute only.
A program may use at most 64 MiB of HBM per device.

```python
import math
import jax
import jax.numpy as jnp
from jax import lax

D = 256
BLOCK = 128
SLOTS = 8
TILES = 1024
ROWS = 131072
OWN_BLOCKS = 32
CAMPAIGNS = 32768
N_CAMP = 8


def draw_imp_emb(key, part):
    base = jax.random.normal(jax.random.fold_in(key, 11), (ROWS, D), jnp.float32)
    base = jnp.clip(base, -6.0, 6.0)
    return base.astype(jnp.bfloat16)


def draw_block_lists(key, part):
    keys = jax.random.split(jax.random.fold_in(key, 23), TILES * N_CAMP)
    picks = jax.vmap(lambda one: jax.random.permutation(one, OWN_BLOCKS)[:SLOTS])(keys)
    return picks.reshape(TILES, N_CAMP, SLOTS).astype(jnp.int32)


def draw_block_counts(key, part):
    heavy = jax.random.randint(jax.random.fold_in(key, 31), (TILES, 1), SLOTS // 2, SLOTS + 1)
    spread = jax.random.randint(jax.random.fold_in(key, 37), (TILES, N_CAMP), 0, SLOTS)
    counts = 1 + spread * heavy // SLOTS
    counts = counts.at[0, :].set(SLOTS)
    return counts.astype(jnp.int32)


def block_levels(own_key, shape, cuts, low, largest):
    def one(dim, parts):
        steps = jax.random.uniform(jax.random.fold_in(jax.random.fold_in(own_key, 6), dim), (parts,), jnp.float32, low / len(cuts), largest / len(cuts))
        return jnp.repeat(jnp.exp(steps), shape[dim] // parts).reshape((-1,) + (1,) * (len(shape) - dim - 1))

    factor_of = one(*cuts[0])
    for cut in cuts[1:]:
        factor_of = factor_of * one(*cut)
    return factor_of


def scatter_about(stream_key, shape, deviation, reach, cuts=(), kind=jnp.bfloat16):
    values = jax.random.normal(stream_key, shape, jnp.float32) * deviation
    if len(cuts) > 0:
        values = block_levels(stream_key, shape, cuts, -0.22, 0.18) * values
    return jnp.clip(values, min=-reach, max=reach).astype(kind)


def setup_inputs(seed: int = 0) -> dict:
    streams_of = jax.random.split(jax.random.key(seed), 8)
    return {
        "imp_emb": draw_imp_emb(jax.random.fold_in(streams_of[7], 71), 0),
        "imp_cost": jnp.clip(jnp.exp(math.log(1.0) - 2.306499 * jax.random.uniform(streams_of[1], (ROWS,), jnp.float32) ** block_levels(streams_of[1], (ROWS,), ((0, 256),), -0.2, 0.2)), 0.099609375, 1.0).astype(jnp.bfloat16),
        "camp_emb": scatter_about(streams_of[2], (CAMPAIGNS, D), 1.0, 6.0, ((0, 256),)),
        "prices": scatter_about(streams_of[3], (CAMPAIGNS,), 1.0, 5.0, ((0, 256),)),
        "spend_limits": jnp.clip(jnp.exp(math.log(64.0) - 2.5494452 * jax.random.uniform(streams_of[4], (CAMPAIGNS,), jnp.float32) ** block_levels(streams_of[4], (CAMPAIGNS,), ((0, 256),), -0.2, 0.2)), 5.0, 64.0),
        "block_lists": draw_block_lists(jax.random.fold_in(streams_of[7], 71), 0),
        "block_counts": draw_block_counts(jax.random.fold_in(streams_of[7], 71), 0),
    }


def reference(imp_emb, imp_cost, camp_emb, prices, spend_limits, block_lists, block_counts):
    scale = 3.0 / jnp.sqrt(jnp.float32(D))
    camp_blocks = camp_emb.reshape(N_CAMP, OWN_BLOCKS, BLOCK, D)
    price_blocks = prices.astype(jnp.float32).reshape(N_CAMP, OWN_BLOCKS, BLOCK)
    tile_emb = imp_emb.reshape(TILES, BLOCK, D)
    tile_cost = imp_cost.astype(jnp.float32).reshape(TILES, BLOCK)
    owners = jnp.arange(N_CAMP, dtype=jnp.int32)[:, None]

    def per_tile(items):
        emb, cost, lists, counts = items
        chosen = camp_blocks[owners, lists].reshape(N_CAMP * SLOTS * BLOCK, D)
        chosen_price = price_blocks[owners, lists]
        raw = jnp.dot(emb, chosen.T, preferred_element_type=jnp.float32)
        logits = raw.reshape(BLOCK, N_CAMP, SLOTS, BLOCK) * scale - chosen_price[None]
        live = (jnp.arange(SLOTS, dtype=jnp.int32)[None, :] < counts[:, None])[None, :, :, None]
        top = lax.optimization_barrier(jnp.max(jnp.where(live, logits, -jnp.inf), axis=(1, 2, 3)))
        expo = jnp.exp(jnp.where(live, logits - top[:, None, None, None], -jnp.inf))
        total = lax.optimization_barrier(jnp.sum(expo, axis=(1, 2, 3)))
        weight = expo / total[:, None, None, None]
        contrib = lax.optimization_barrier(jnp.sum(weight * cost[:, None, None, None], axis=0))
        return (contrib, top + jnp.log(total))
    contribs, logz = lax.map(per_tile, (tile_emb, tile_cost, block_lists, block_counts))
    owner_idx = jnp.broadcast_to(jnp.arange(N_CAMP, dtype=jnp.int32)[None, :, None], block_lists.shape)
    spend = jnp.zeros((N_CAMP, OWN_BLOCKS, BLOCK), jnp.float32).at[owner_idx, block_lists].add(contribs)
    spend = spend.reshape(CAMPAIGNS)
    new_prices = prices.astype(jnp.float32) + 2.0 * (spend - spend_limits) / (spend + spend_limits)
    return (new_prices, logz.reshape(ROWS))
```

```python
import functools
import math

import jax
import jax.numpy as jnp
from jax import lax
from jax.experimental import pallas as pl
from jax.experimental.pallas import tpu as pltpu
from jax.sharding import PartitionSpec as P

D = 256
BLOCK = 128
SLOTS = 8
NZ, NY, NX, NC = 8, 4, 4, 2
OWN = NZ * NY
TILES = 32
DEAD = OWN
PAD = 16
CBLK = BLOCK + PAD
LOG2E = math.log2(math.e)
LN2 = math.log(2.0)
SCALE2 = 3.0 / math.sqrt(D) * LOG2E
VMEM_LIMIT = 56 * 1024 * 1024


def shift_z(v, k):
    perm = [(z * NY + y, (z + k) % NZ * NY + y) for z in range(NZ) for y in range(NY)]
    return lax.ppermute(v, "imp", perm)


def shift_y(v, k):
    perm = [(z * NY + y, z * NY + (y + k) % NY) for z in range(NZ) for y in range(NY)]
    return lax.ppermute(v, "imp", perm)


def shift_x(v, k):
    perm = [(x * NC + c, (x + k) % NX * NC + c) for x in range(NX) for c in range(NC)]
    return lax.ppermute(v, "camp", perm)


def other_core(v):
    perm = [(x * NC + c, x * NC + 1 - c) for x in range(NX) for c in range(NC)]
    return lax.ppermute(v, "camp", perm)


PAIR_DZ = (0, 4)
REST_DZ = (7, 3, 1, 5, 6, 2)
DY = (0, 3, 1, 2)
DX = (0, 3, 1, 2)


def scores(tab, pb, rows_t, b):
    raw = lax.dot_general(tab[b], rows_t, (((1,), (1,)), ((), ())), preferred_element_type=jnp.float32)
    return raw * SCALE2 - pb[b]


def by_count(count, body):
    for hi in (2, 4, 6, 8):
        pl.when((count > hi - 2) & (count <= hi))(functools.partial(body, hi))


def fold(v):
    return v.reshape(v.shape[0] // 8, 8, v.shape[1])


def stats_kernel(ids, counts, where, *refs):
    rows_in, pairs, rests = refs[:8], refs[8:12], refs[12:16]
    stat, rows, tab, pb, sbuf = refs[16:]
    z, y, x, core = where[0], where[1], where[2], where[3]
    eye = lax.broadcasted_iota(jnp.int32, (BLOCK, BLOCK), 0) == lax.broadcasted_iota(jnp.int32, (BLOCK, BLOCK), 1)
    ones = jnp.ones((BLOCK, BLOCK), jnp.bfloat16)
    for bufs, offsets in ((pairs, PAIR_DZ), (rests, REST_DZ)):
        for buf, dy in zip(bufs, DY):
            for i, dz in enumerate(offsets):
                b = lax.rem(z + dz, NZ) * NY + lax.rem(y + dy, NY)
                tab[b] = buf[i * CBLK : i * CBLK + BLOCK, :]
                row = buf[i * CBLK + BLOCK : (i + 1) * CBLK, :][0:1, 0:BLOCK].astype(jnp.float32)
                diag = jnp.where(eye, jnp.broadcast_to(row, (BLOCK, BLOCK)), 0.0).astype(jnp.bfloat16)
                pb[b] = jnp.dot(diag, ones, preferred_element_type=jnp.float32) * LOG2E
    tab[DEAD] = jnp.zeros((BLOCK, D), jnp.bfloat16)
    pb[DEAD] = jnp.full((BLOCK, BLOCK), jnp.inf, jnp.float32)
    for k in range(8):
        xs = lax.rem(x + DX[k % 4], NX)
        cs = core if k < 4 else 1 - core
        for j in range(4):
            rows[(xs * NC + cs) * 4 + j] = rows_in[k][j * BLOCK : (j + 1) * BLOCK, :]

    def tile(t, carry):
        def body(n):
            rows_t = rows[t]
            top = None
            for s in range(n):
                logit = scores(tab, pb, rows_t, ids[t, s])
                sbuf[s] = logit
                part = jnp.max(fold(logit), axis=0)
                top = part if top is None else jnp.maximum(top, part)
            top = jnp.max(top, axis=0, keepdims=True)
            total = jnp.zeros((8, BLOCK), jnp.float32)
            for s in range(n):
                total = total + jnp.sum(fold(jnp.exp2(sbuf[s] - top)), axis=0)
            stat[pl.ds(t, 1), :] = top
            stat[pl.ds(TILES + t, 1), :] = jnp.sum(total, axis=0, keepdims=True)

        by_count(counts[t], body)
        return carry

    lax.fori_loop(0, TILES, tile, 0)


def spend_kernel(ids, counts, s0, s1, s2, s3, cost, rows, tab, pb, spend, logz, acc, topw):
    stats = (s0, s1, s2, s3)
    top = functools.reduce(jnp.maximum, [s[0:TILES, :] for s in stats])
    total = sum(s[TILES:, :] * jnp.exp2(s[0:TILES, :] - top) for s in stats)
    logz[...] = (top + jnp.log2(total)) * LN2
    topw[0:TILES, :] = top
    topw[TILES:, :] = cost[...] / total
    for b in range(OWN):
        acc[b] = jnp.zeros((BLOCK, BLOCK), jnp.float32)

    def tile(t, carry):
        def body(n):
            rows_t = rows[t]
            top_t = topw[pl.ds(t, 1), :]
            w_t = topw[pl.ds(TILES + t, 1), :]
            out = []
            for s in range(n):
                e = jnp.exp2(scores(tab, pb, rows_t, ids[t, s]) - top_t) * w_t
                out.append(acc[ids[t, s]] + e)
            for s in range(n):
                acc[ids[t, s]] = out[s]

        by_count(counts[t], body)
        return carry

    lax.fori_loop(0, TILES, tile, 0)
    for b in range(OWN):
        spend[b : b + 1, :] = jnp.sum(acc[b].T, axis=0, keepdims=True)


VM = pl.BlockSpec(memory_space=pltpu.VMEM)
SM = pl.BlockSpec(memory_space=pltpu.SMEM)


def local(imp_emb, imp_cost, camp_emb, prices, spend_limits, block_lists, block_counts):
    imp, camp = lax.axis_index("imp"), lax.axis_index("camp")
    where = jnp.stack([imp // NY, imp % NY, camp // NC, camp % NC]).astype(jnp.int32)
    counts = block_counts[:, 0]
    ids = jnp.where(jnp.arange(SLOTS, dtype=jnp.int32)[None, :] < counts[:, None], block_lists[:, 0, :], DEAD)

    blk = jnp.concatenate([camp_emb, jnp.pad(prices.reshape(1, BLOCK), ((0, PAD - 1), (0, D - BLOCK)))], 0)
    pair = jnp.concatenate([blk, shift_z(blk, 4)], 0)
    own = jnp.concatenate([imp_emb, jnp.pad(imp_cost.reshape(2, D), ((0, PAD - 2), (0, 0)))], 0)
    rows_in = [own] + [shift_x(own, k) for k in (1, -1, 2)]
    rest = jnp.concatenate([shift_z(pair, 1), shift_z(pair, -1), shift_z(pair, 2)], 0)
    pairs = [pair] + [shift_y(pair, k) for k in (1, -1, 2)]
    rests = [rest] + [shift_y(rest, k) for k in (1, -1, 2)]
    rows_in = rows_in + [other_core(v) for v in rows_in]

    stat, rows, tab, pb = pl.pallas_call(
        stats_kernel,
        in_specs=[SM] * 3 + [VM] * 16,
        out_specs=[VM] * 4,
        out_shape=[
            jax.ShapeDtypeStruct((2 * TILES, BLOCK), jnp.float32),
            jax.ShapeDtypeStruct((TILES, BLOCK, D), jnp.bfloat16),
            jax.ShapeDtypeStruct((OWN + 1, BLOCK, D), jnp.bfloat16),
            jax.ShapeDtypeStruct((OWN + 1, BLOCK, BLOCK), jnp.float32),
        ],
        scratch_shapes=[pltpu.VMEM((SLOTS, BLOCK, BLOCK), jnp.float32)],
        compiler_params=pltpu.CompilerParams(vmem_limit_bytes=VMEM_LIMIT),
        name="stats",
    )(ids, counts, where, *rows_in, *pairs, *rests)

    xs = [(camp // NC + d) % NX for d in DX]
    order = jnp.stack([x * NC + camp % NC for x in xs] + [x * NC + 1 - camp % NC for x in xs])
    cost_in = jnp.stack([v[512:514, :].reshape(4, BLOCK) for v in rows_in]).astype(jnp.float32)
    onehot = order[None, :] == jnp.arange(8)[:, None]
    cost = jnp.sum(jnp.where(onehot[:, :, None, None], cost_in[None], 0.0), axis=1).reshape(TILES, BLOCK)

    far = other_core(stat)
    m0, m1 = stat[:TILES], far[:TILES]
    m = jnp.maximum(m0, m1)
    both = jnp.concatenate([m, stat[TILES:] * jnp.exp2(m0 - m) + far[TILES:] * jnp.exp2(m1 - m)], 0)
    all_stats = [both] + [shift_x(both, k) for k in (1, -1, 2)]

    spend, logz = pl.pallas_call(
        spend_kernel,
        in_specs=[SM] * 2 + [VM] * 8,
        out_specs=[VM] * 2,
        out_shape=[jax.ShapeDtypeStruct((TILES, BLOCK), jnp.float32)] * 2,
        scratch_shapes=[
            pltpu.VMEM((OWN + 1, BLOCK, BLOCK), jnp.float32),
            pltpu.VMEM((2 * TILES, BLOCK), jnp.float32),
        ],
        compiler_params=pltpu.CompilerParams(vmem_limit_bytes=VMEM_LIMIT),
        name="spend",
    )(ids, counts, *all_stats, cost, rows, tab, pb)

    mine = jnp.sum(lax.all_to_all(spend, "imp", 0, 0), axis=0)
    new_prices = prices.astype(jnp.float32) + 2.0 * (mine - spend_limits) / (mine + spend_limits)
    return (new_prices, logz.reshape(TILES * BLOCK))


def solution(mesh):
    return jax.shard_map(
        local,
        mesh=mesh,
        in_specs=(
            P(("imp", "camp"), None),
            P(("imp", "camp")),
            P(("camp", "imp"), None),
            P(("camp", "imp")),
            P(("camp", "imp")),
            P("imp", "camp", None),
            P("imp", "camp"),
        ),
        out_specs=(P(("camp", "imp")), P("imp")),
        check_vma=False,
    )
```

```python
import functools
import math

import jax
import jax.numpy as jnp
from jax import lax
from jax.experimental import pallas as pl
from jax.experimental.pallas import tpu as pltpu
from jax.sharding import PartitionSpec as P

D = 256
BLOCK = 128
SLOTS = 8
NZ, NY, NX, NC = 8, 4, 4, 2
OWN = NZ * NY
TILES = 32
DEAD = OWN
PAD = 16
CBLK = BLOCK + PAD
LOG2E = math.log2(math.e)
LN2 = math.log(2.0)
SCALE2 = 3.0 / math.sqrt(D) * LOG2E
VMEM_LIMIT = 24 * 1024 * 1024
UNROLL = 4
GROUPS = TILES * SLOTS // 2 + UNROLL
LAST = GROUPS
TRASH = TILES * SLOTS
LOWEST = -3e38


def shift_z(v, k):
    perm = [(z * NY + y, (z + k) % NZ * NY + y) for z in range(NZ) for y in range(NY)]
    return lax.ppermute(v, "imp", perm)


def shift_y(v, k):
    perm = [(z * NY + y, z * NY + (y + k) % NY) for z in range(NZ) for y in range(NY)]
    return lax.ppermute(v, "imp", perm)


def shift_x(v, k):
    perm = [(x * NC + c, (x + k) % NX * NC + c) for x in range(NX) for c in range(NC)]
    return lax.ppermute(v, "camp", perm)


def other_core(v):
    perm = [(x * NC + c, x * NC + 1 - c) for x in range(NX) for c in range(NC)]
    return lax.ppermute(v, "camp", perm)


PAIR_DZ = (0, 4)
REST_DZ = (7, 3, 1, 5, 6, 2)
DY = (0, 3, 1, 2)
DX = (0, 3, 1, 2)


def fold(v):
    return v.reshape(v.shape[0] // 8, 8, v.shape[1])


def prep_kernel(lists, counts, where, *refs):
    rows_in = refs[:8]
    rows, cost, groups = refs[8:]
    x, core = where[2], where[3]
    for k in range(8):
        xs = lax.rem(x + DX[k % 4], NX)
        cs = core if k < 4 else 1 - core
        first = (xs * NC + cs) * 4
        extra = rows_in[k][4 * BLOCK :, :].astype(jnp.float32)
        for j in range(4):
            rows[first + j] = rows_in[k][j * BLOCK : (j + 1) * BLOCK, :]
            cost[pl.ds(first + j, 1), :] = extra[j // 2 : j // 2 + 1, j % 2 * BLOCK : (j % 2 + 1) * BLOCK]

    def tile(t, at):
        count = counts[t]

        def group(j, at):
            groups[0, at] = t
            groups[1, at] = t * SLOTS + 2 * j
            groups[2, at] = lists[t, 2 * j]
            groups[3, at] = jnp.where(2 * j + 1 < count, lists[t, 2 * j + 1], DEAD)
            return at + 1

        return lax.fori_loop(0, (count + 1) // 2, group, at)

    end = lax.fori_loop(0, TILES, tile, 0)
    for j in range(UNROLL):
        groups[0, end + j] = 0
        groups[1, end + j] = TRASH
        groups[2, end + j] = DEAD
        groups[3, end + j] = DEAD
    groups[0, LAST] = (end + UNROLL - 1) // UNROLL


def stats_kernel(groups, where, *refs):
    rows, pairs, rests = refs[0], refs[1:5], refs[5:9]
    stat, expo, tops, tab, pb, totals = refs[9:]
    z, y = where[0], where[1]
    eye = lax.broadcasted_iota(jnp.int32, (BLOCK, BLOCK), 0) == lax.broadcasted_iota(jnp.int32, (BLOCK, BLOCK), 1)
    ones = jnp.ones((BLOCK, BLOCK), jnp.bfloat16)
    for bufs, offsets in ((pairs, PAIR_DZ), (rests, REST_DZ)):
        for buf, dy in zip(bufs, DY):
            for i, dz in enumerate(offsets):
                b = lax.rem(z + dz, NZ) * NY + lax.rem(y + dy, NY)
                tab[b] = buf[i * CBLK : i * CBLK + BLOCK, :]
                row = buf[i * CBLK + BLOCK : (i + 1) * CBLK, :][0:1, 0:BLOCK].astype(jnp.float32)
                diag = jnp.where(eye, jnp.broadcast_to(row, (BLOCK, BLOCK)), 0.0).astype(jnp.bfloat16)
                pb[b] = jnp.dot(diag, ones, preferred_element_type=jnp.float32) * LOG2E
    tab[DEAD] = jnp.zeros((BLOCK, D), jnp.bfloat16)
    pb[DEAD] = jnp.full((BLOCK, BLOCK), -LOWEST, jnp.float32)
    for p in range(TILES * SLOTS):
        tops[p] = jnp.full((8, BLOCK), LOWEST, jnp.float32)
        totals[p] = jnp.zeros((8, BLOCK), jnp.float32)

    def step(i, carry):
        for u in range(UNROLL):
            g = i * UNROLL + u
            rows_t = rows[groups[0, g]]
            for k in range(2):
                b = groups[2 + k, g]
                raw = lax.dot_general(tab[b], rows_t, (((1,), (1,)), ((), ())), preferred_element_type=jnp.float32)
                logit = fold(raw * SCALE2 - pb[b])
                top = jnp.max(logit, axis=0)
                e = jnp.exp2(logit - top[None])
                expo[2 * g + k] = e.reshape(BLOCK, BLOCK)
                tops[groups[1, g] + k] = top
                totals[groups[1, g] + k] = jnp.sum(e, axis=0)
        return carry

    lax.fori_loop(0, groups[0, LAST], step, 0)

    for t in range(TILES):
        top_s = [tops[t * SLOTS + s] for s in range(SLOTS)]
        top8 = functools.reduce(jnp.maximum, top_s)
        top = jnp.max(top8, axis=0, keepdims=True)
        total8 = sum(totals[t * SLOTS + s] * jnp.exp2(top_s[s] - top) for s in range(SLOTS))
        total = jnp.sum(total8, axis=0, keepdims=True)
        for c in range(NX * NC):
            stat[c, t : t + 1, :] = top
            stat[c, TILES + t : TILES + t + 1, :] = total


def spend_kernel(groups, stats, cost, expo, tops, spend, logz, acc, topw):
    owners = NX * NC
    top = functools.reduce(jnp.maximum, [stats[c, 0:TILES, :] for c in range(owners)])
    total = sum(stats[c, TILES:, :] * jnp.exp2(stats[c, 0:TILES, :] - top) for c in range(owners))
    logz[...] = (top + jnp.log2(total)) * LN2
    topw[0:TILES, :] = top
    topw[TILES:, :] = cost[...] / total
    for b in range(OWN):
        acc[b] = jnp.zeros((BLOCK, BLOCK), jnp.float32)

    def step(i, carry):
        for u in range(UNROLL):
            g = i * UNROLL + u
            t = groups[0, g]
            top_t = topw[pl.ds(t, 1), :]
            w_t = topw[pl.ds(TILES + t, 1), :]
            for k in range(2):
                factor = jnp.exp2(tops[groups[1, g] + k] - top_t) * w_t
                b = groups[2 + k, g]
                part = fold(expo[2 * g + k]) * factor[None]
                acc[b] = acc[b] + part.reshape(BLOCK, BLOCK)
        return carry

    lax.fori_loop(0, groups[0, LAST], step, 0)
    for b in range(OWN):
        spend[b : b + 1, :] = jnp.sum(acc[b].T, axis=0, keepdims=True)


VM = pl.BlockSpec(memory_space=pltpu.VMEM)
SM = pl.BlockSpec(memory_space=pltpu.SMEM)
OUT = pltpu.VMEM


def local(imp_emb, imp_cost, camp_emb, prices, spend_limits, block_lists, block_counts):
    imp, camp = lax.axis_index("imp"), lax.axis_index("camp")
    where = jnp.stack([imp // NY, imp % NY, camp // NC, camp % NC]).astype(jnp.int32)

    blk = jnp.concatenate([camp_emb, jnp.pad(prices.reshape(1, BLOCK), ((0, PAD - 1), (0, D - BLOCK)))], 0)
    pair = jnp.concatenate([blk, shift_z(blk, 4)], 0)
    own = jnp.concatenate([imp_emb, jnp.pad(imp_cost.reshape(2, D), ((0, PAD - 2), (0, 0)))], 0)
    rows_in = [own] + [shift_x(own, k) for k in (1, -1, 2)]
    rest = jnp.concatenate([shift_z(pair, 1), shift_z(pair, -1), shift_z(pair, 2)], 0)
    pairs = [pair] + [shift_y(pair, k) for k in (1, -1, 2)]
    rests = [rest] + [shift_y(rest, k) for k in (1, -1, 2)]
    rows_in = rows_in + [other_core(v) for v in rows_in]

    params = pltpu.CompilerParams(vmem_limit_bytes=VMEM_LIMIT)
    rows, cost, groups = pl.pallas_call(
        prep_kernel,
        in_specs=[SM] * 3 + [VM] * 8,
        out_specs=[VM, VM, SM],
        out_shape=[
            OUT((TILES, BLOCK, D), jnp.bfloat16),
            OUT((TILES, BLOCK), jnp.float32),
            jax.ShapeDtypeStruct((4, GROUPS + 1), jnp.int32),
        ],
        compiler_params=params,
        name="prep",
    )(block_lists[:, 0, :], block_counts[:, 0], where, *rows_in)

    stat, expo, tops = pl.pallas_call(
        stats_kernel,
        in_specs=[SM] * 2 + [VM] * 9,
        out_specs=[VM] * 3,
        out_shape=[
            OUT((NX * NC, 2 * TILES, BLOCK), jnp.float32),
            OUT((2 * GROUPS, BLOCK, BLOCK), jnp.float32),
            OUT((TRASH + 2, 8, BLOCK), jnp.float32),
        ],
        scratch_shapes=[
            pltpu.VMEM((OWN + 1, BLOCK, D), jnp.bfloat16),
            pltpu.VMEM((OWN + 1, BLOCK, BLOCK), jnp.float32),
            pltpu.VMEM((TRASH + 2, 8, BLOCK), jnp.float32),
        ],
        compiler_params=params,
        name="stats",
    )(groups, where, rows, *pairs, *rests)

    stats = lax.all_to_all(stat, "camp", 0, 0)

    spend, logz = pl.pallas_call(
        spend_kernel,
        in_specs=[SM] + [VM] * 4,
        out_specs=[VM] * 2,
        out_shape=[
            OUT((OWN, BLOCK), jnp.float32),
            jax.ShapeDtypeStruct((TILES, BLOCK), jnp.float32),
        ],
        scratch_shapes=[
            pltpu.VMEM((OWN + 1, BLOCK, BLOCK), jnp.float32),
            pltpu.VMEM((2 * TILES, BLOCK), jnp.float32),
        ],
        compiler_params=params,
        name="spend",
    )(groups, stats, cost, expo, tops)

    mine = jnp.sum(lax.all_to_all(spend, "imp", 0, 0), axis=0)
    new_prices = prices.astype(jnp.float32) + 2.0 * (mine - spend_limits) / (mine + spend_limits)
    return (new_prices, logz.reshape(TILES * BLOCK))


def solution(mesh):
    return jax.shard_map(
        local,
        mesh=mesh,
        in_specs=(
            P(("imp", "camp"), None),
            P(("imp", "camp")),
            P(("camp", "imp"), None),
            P(("camp", "imp")),
            P(("camp", "imp")),
            P("imp", "camp", None),
            P("imp", "camp"),
        ),
        out_specs=(P(("camp", "imp")), P("imp")),
        check_vma=False,
    )
```

```python
import functools
import math

import jax
import jax.numpy as jnp
from jax import lax
from jax.experimental import pallas as pl
from jax.experimental.pallas import tpu as pltpu
from jax.sharding import PartitionSpec as P

D = 256
BLOCK = 128
SLOTS = 8
NZ, NY, NX, NC = 8, 4, 4, 2
OWN = NZ * NY
TILES = 32
DEAD = OWN
PAD = 16
CBLK = BLOCK + PAD
LOG2E = math.log2(math.e)
LN2 = math.log(2.0)
SCALE2 = 3.0 / math.sqrt(D) * LOG2E
VMEM_LIMIT = 16 * 1024 * 1024
UNROLL = 4
GROUPS = TILES * SLOTS // 2 + UNROLL
LAST = GROUPS
TRASH = TILES * SLOTS
LOWEST = -3e38


def shift_z(v, k):
    perm = [(z * NY + y, (z + k) % NZ * NY + y) for z in range(NZ) for y in range(NY)]
    return lax.ppermute(v, "imp", perm)


def shift_y(v, k):
    perm = [(z * NY + y, z * NY + (y + k) % NY) for z in range(NZ) for y in range(NY)]
    return lax.ppermute(v, "imp", perm)


def shift_x(v, k):
    perm = [(x * NC + c, (x + k) % NX * NC + c) for x in range(NX) for c in range(NC)]
    return lax.ppermute(v, "camp", perm)


def other_core(v):
    perm = [(x * NC + c, x * NC + 1 - c) for x in range(NX) for c in range(NC)]
    return lax.ppermute(v, "camp", perm)


NEAR, FAR = (7, 3, 1, 5), (0, 4, 6, 2)
LAYOUT = ((0, NEAR), (0, FAR), (3, NEAR), (1, NEAR), (3, FAR), (1, FAR), (2, NEAR), (2, FAR))
DX = (0, 3, 1, 2)


def fold(v):
    return v.reshape(v.shape[0] // 8, 8, v.shape[1])


def prep_kernel(lists, counts, groups):
    def tile(t, at):
        count = counts[t]

        def group(j, at):
            groups[0, at] = t
            groups[1, at] = t * SLOTS + 2 * j
            groups[2, at] = lists[t, 2 * j]
            groups[3, at] = jnp.where(2 * j + 1 < count, lists[t, 2 * j + 1], DEAD)
            return at + 1

        return lax.fori_loop(0, (count + 1) // 2, group, at)

    end = lax.fori_loop(0, TILES, tile, 0)
    for j in range(UNROLL):
        groups[0, end + j] = 0
        groups[1, end + j] = TRASH
        groups[2, end + j] = DEAD
        groups[3, end + j] = DEAD
    groups[0, LAST] = (end + UNROLL - 1) // UNROLL


def stats_kernel(groups, where, *refs):
    rows_in, camps = refs[:8], refs[8:16]
    stat, cost, expo, tops, rows, extra, tab, pb, totals, sems = refs[16:]
    z, y, x, core = where[0], where[1], where[2], where[3]
    copies = []
    for k in range(8):
        q = lax.rem(x + DX[k % 4], NX) * NC + (core if k < 4 else 1 - core)
        whole = rows.at[pl.ds(pl.multiple_of(q * 512, 512), 512), :]
        rest = extra.at[pl.ds(pl.multiple_of(q * PAD, PAD), PAD), :]
        copies.append(pltpu.make_async_copy(rows_in[k].at[0:512, :], whole, sems.at[k]))
        copies.append(pltpu.make_async_copy(rows_in[k].at[512:528, :], rest, sems.at[8 + k]))
    for copy in copies:
        copy.start()
    eye = lax.broadcasted_iota(jnp.int32, (BLOCK, BLOCK), 0) == lax.broadcasted_iota(jnp.int32, (BLOCK, BLOCK), 1)
    ones = jnp.ones((BLOCK, BLOCK), jnp.bfloat16)
    for buf, (dy, offsets) in zip(camps, LAYOUT):
        for i, dz in enumerate(offsets):
            b = lax.rem(z + dz, NZ) * NY + lax.rem(y + dy, NY)
            tab[b] = buf[i * CBLK : i * CBLK + BLOCK, :]
            row = buf[i * CBLK + BLOCK : (i + 1) * CBLK, :][0:1, 0:BLOCK].astype(jnp.float32)
            diag = jnp.where(eye, jnp.broadcast_to(row, (BLOCK, BLOCK)), 0.0).astype(jnp.bfloat16)
            pb[b] = jnp.dot(diag, ones, preferred_element_type=jnp.float32) * LOG2E
    tab[DEAD] = jnp.zeros((BLOCK, D), jnp.bfloat16)
    pb[DEAD] = jnp.full((BLOCK, BLOCK), -LOWEST, jnp.float32)
    for p in range(TILES * SLOTS):
        tops[p] = jnp.full((8, BLOCK), LOWEST, jnp.float32)
        totals[p] = jnp.zeros((8, BLOCK), jnp.float32)
    for copy in copies:
        copy.wait()
    for q in range(NX * NC):
        two = extra[q * PAD : (q + 1) * PAD, :].astype(jnp.float32)
        for j in range(4):
            cost[4 * q + j : 4 * q + j + 1, :] = two[j // 2 : j // 2 + 1, j % 2 * BLOCK : (j % 2 + 1) * BLOCK]

    def step(i, carry):
        for u in range(UNROLL):
            g = i * UNROLL + u
            rows_t = rows[pl.ds(pl.multiple_of(groups[0, g] * BLOCK, BLOCK), BLOCK), :]
            for k in range(2):
                b = groups[2 + k, g]
                raw = lax.dot_general(tab[b], rows_t, (((1,), (1,)), ((), ())), preferred_element_type=jnp.float32)
                logit = fold(raw * SCALE2 - pb[b])
                top = jnp.max(logit, axis=0)
                e = jnp.exp2(logit - top[None])
                expo[2 * g + k] = e.reshape(BLOCK, BLOCK)
                tops[groups[1, g] + k] = top
                totals[groups[1, g] + k] = jnp.sum(e, axis=0)
        return carry

    lax.fori_loop(0, groups[0, LAST], step, 0)

    for t in range(TILES):
        top_s = [tops[t * SLOTS + s] for s in range(SLOTS)]
        top8 = functools.reduce(jnp.maximum, top_s)
        top = jnp.max(top8, axis=0, keepdims=True)
        total8 = sum(totals[t * SLOTS + s] * jnp.exp2(top_s[s] - top) for s in range(SLOTS))
        total = jnp.sum(total8, axis=0, keepdims=True)
        for c in range(NX * NC):
            stat[c, t : t + 1, :] = top
            stat[c, TILES + t : TILES + t + 1, :] = total


def spend_kernel(groups, stats, cost, expo, tops, spend, logz, acc, topw):
    owners = NX * NC
    top = functools.reduce(jnp.maximum, [stats[c, 0:TILES, :] for c in range(owners)])
    total = sum(stats[c, TILES:, :] * jnp.exp2(stats[c, 0:TILES, :] - top) for c in range(owners))
    logz[...] = (top + jnp.log2(total)) * LN2
    topw[0:TILES, :] = top
    topw[TILES:, :] = cost[...] / total
    for b in range(OWN):
        acc[b] = jnp.zeros((BLOCK, BLOCK), jnp.float32)

    def step(i, carry):
        for u in range(UNROLL):
            g = i * UNROLL + u
            t = groups[0, g]
            top_t = topw[pl.ds(t, 1), :]
            w_t = topw[pl.ds(TILES + t, 1), :]
            for k in range(2):
                factor = jnp.exp2(tops[groups[1, g] + k] - top_t) * w_t
                b = groups[2 + k, g]
                part = fold(expo[2 * g + k]) * factor[None]
                acc[b] = acc[b] + part.reshape(BLOCK, BLOCK)
        return carry

    lax.fori_loop(0, groups[0, LAST], step, 0)
    for b in range(OWN):
        spend[b : b + 1, :] = jnp.sum(acc[b].T, axis=0, keepdims=True)


VM = pl.BlockSpec(memory_space=pltpu.VMEM)
SM = pl.BlockSpec(memory_space=pltpu.SMEM)
OUT = pltpu.VMEM


def local(imp_emb, imp_cost, camp_emb, prices, spend_limits, block_lists, block_counts):
    imp, camp = lax.axis_index("imp"), lax.axis_index("camp")
    where = jnp.stack([imp // NY, imp % NY, camp // NC, camp % NC]).astype(jnp.int32)

    params = pltpu.CompilerParams(vmem_limit_bytes=VMEM_LIMIT)
    groups = pl.pallas_call(
        prep_kernel,
        in_specs=[SM] * 2,
        out_specs=SM,
        out_shape=jax.ShapeDtypeStruct((4, GROUPS + 1), jnp.int32),
        name="prep",
    )(block_lists[:, 0, :], block_counts[:, 0])

    blk = jnp.concatenate([camp_emb, jnp.pad(prices.reshape(1, BLOCK), ((0, PAD - 1), (0, D - BLOCK)))], 0)
    own = jnp.concatenate([imp_emb, jnp.pad(imp_cost.reshape(2, D), ((0, PAD - 2), (0, 0)))], 0)
    blk4 = shift_z(blk, 4)
    near = other_core(own)
    blk4, own1 = lax.optimization_barrier((blk4, own))
    pair = jnp.concatenate([blk, blk4], 0)
    up, down, two = shift_z(pair, 1), shift_z(pair, -1), shift_z(pair, 2)
    left, right = shift_x(own1, 1), shift_x(own1, -1)
    across = shift_x(own1, 2)
    a, b = jnp.concatenate([up, down], 0), jnp.concatenate([pair, two], 0)
    a_up, b_down = shift_y(a, 1), shift_y(b, -1)
    b_up, a_down = shift_y(b, 1), shift_y(a, -1)
    a_up, b_down, left, right, across, groups = lax.optimization_barrier((a_up, b_down, left, right, across, groups))
    a_two, b_two = shift_y(a_up, 1), shift_y(b_down, -1)
    rows_in = [own, left, right, across, near, other_core(left), other_core(right), other_core(across)]
    camps = [a, b, a_up, a_down, b_up, b_down, a_two, b_two]

    stat, cost, expo, tops = pl.pallas_call(
        stats_kernel,
        in_specs=[SM] * 2 + [pl.BlockSpec(memory_space=pl.ANY)] * 8 + [VM] * 8,
        out_specs=[VM] * 4,
        out_shape=[
            OUT((NX * NC, 2 * TILES, BLOCK), jnp.float32),
            OUT((TILES, BLOCK), jnp.float32),
            OUT((2 * GROUPS, BLOCK, BLOCK), jnp.float32),
            OUT((TRASH + 2, 8, BLOCK), jnp.float32),
        ],
        scratch_shapes=[
            pltpu.VMEM((TILES * BLOCK, D), jnp.bfloat16),
            pltpu.VMEM((NX * NC * PAD, D), jnp.bfloat16),
            pltpu.VMEM((OWN + 1, BLOCK, D), jnp.bfloat16),
            pltpu.VMEM((OWN + 1, BLOCK, BLOCK), jnp.float32),
            pltpu.VMEM((TRASH + 2, 8, BLOCK), jnp.float32),
            pltpu.SemaphoreType.DMA((16,)),
        ],
        compiler_params=params,
        name="stats",
    )(groups, where, *rows_in, *(pltpu.with_memory_space_constraint(v, pltpu.VMEM) for v in camps))

    stats = lax.all_to_all(stat, "camp", 0, 0)

    spend, logz = pl.pallas_call(
        spend_kernel,
        in_specs=[SM] + [VM] * 4,
        out_specs=[VM] * 2,
        out_shape=[
            OUT((OWN, BLOCK), jnp.float32),
            jax.ShapeDtypeStruct((TILES, BLOCK), jnp.float32),
        ],
        scratch_shapes=[
            pltpu.VMEM((OWN + 1, BLOCK, BLOCK), jnp.float32),
            pltpu.VMEM((2 * TILES, BLOCK), jnp.float32),
        ],
        compiler_params=params,
        name="spend",
    )(groups, stats, cost, expo, tops)

    mine = jnp.sum(lax.all_to_all(spend, "imp", 0, 0), axis=0)
    new_prices = prices.astype(jnp.float32) + 2.0 * (mine - spend_limits) / (mine + spend_limits)
    return (new_prices, logz.reshape(TILES * BLOCK))


def solution(mesh):
    return jax.shard_map(
        local,
        mesh=mesh,
        in_specs=(
            P(("imp", "camp"), None),
            P(("imp", "camp")),
            P(("camp", "imp"), None),
            P(("camp", "imp")),
            P(("camp", "imp")),
            P("imp", "camp", None),
            P("imp", "camp"),
        ),
        out_specs=(P(("camp", "imp")), P("imp")),
        check_vma=False,
    )
```

```python
import functools
import math

import jax
import jax.numpy as jnp
from jax import lax
from jax.experimental import pallas as pl
from jax.experimental.pallas import tpu as pltpu
from jax.sharding import PartitionSpec as P

D = 256
BLOCK = 128
SLOTS = 8
NZ, NY, NX, NC = 8, 4, 4, 2
OWN = NZ * NY
TILES = 32
DEAD = OWN
PAD = 16
CBLK = BLOCK + PAD
LOG2E = math.log2(math.e)
LN2 = math.log(2.0)
SCALE2 = 3.0 / math.sqrt(D) * LOG2E
VMEM_LIMIT = 16 * 1024 * 1024
UNROLL = 4
GROUPS = TILES * SLOTS // 2 + UNROLL
LAST = GROUPS
FIRST, SECOND = 1024, 1024 * 64
TRASH = TILES * SLOTS
LOWEST = -3e38


def shift_z(v, k):
    perm = [(z * NY + y, (z + k) % NZ * NY + y) for z in range(NZ) for y in range(NY)]
    return lax.ppermute(v, "imp", perm)


def shift_y(v, k):
    perm = [(z * NY + y, z * NY + (y + k) % NY) for z in range(NZ) for y in range(NY)]
    return lax.ppermute(v, "imp", perm)


def shift_x(v, k):
    perm = [(x * NC + c, (x + k) % NX * NC + c) for x in range(NX) for c in range(NC)]
    return lax.ppermute(v, "camp", perm)


def other_core(v):
    perm = [(x * NC + c, x * NC + 1 - c) for x in range(NX) for c in range(NC)]
    return lax.ppermute(v, "camp", perm)


NEAR, FAR = (7, 3, 1, 5), (0, 4, 6, 2)
LAYOUT = ((0, NEAR), (0, FAR), (3, NEAR), (1, NEAR), (3, FAR), (1, FAR), (2, NEAR), (2, FAR))
DX = (0, 3, 1, 2)


def fold(v):
    return v.reshape(v.shape[0] // 8, 8, v.shape[1])


def prep_kernel(lists, counts, groups):
    def tile(t, at):
        count = counts[t]
        for j in range(SLOTS // 2):
            second = jnp.where(2 * j + 1 < count, lists[2 * j + 1, t], DEAD)
            groups[at] = t * SLOTS + 2 * j + lists[2 * j, t] * FIRST + second * SECOND
            at = at + (2 * j < count).astype(jnp.int32)
        return at

    end = lax.fori_loop(0, TILES, tile, 0)
    for j in range(UNROLL):
        groups[end + j] = TRASH + DEAD * FIRST + DEAD * SECOND
    groups[LAST] = (end + UNROLL - 1) // UNROLL


def unpack(group):
    slot = group & (FIRST - 1)
    return slot, (slot >> 3) & (TILES - 1), ((group >> 10) & 63, group >> 16)


def stats_kernel(groups, where, *refs):
    rows_in, camps, cost = refs[:8], refs[8:16], refs[16]
    stat, expo, tops, rows, tab, pb, totals, sems = refs[17:]
    z, y, x, core = where[0], where[1], where[2], where[3]
    copies = []
    for k in range(8):
        q = lax.rem(x + DX[k % 4], NX) * NC + (core if k < 4 else 1 - core)
        whole = rows.at[pl.ds(pl.multiple_of(q * 512, 512), 512), :]
        copies.append(pltpu.make_async_copy(rows_in[k], whole, sems.at[k]))
    for copy in copies:
        copy.start()
    eye = lax.broadcasted_iota(jnp.int32, (BLOCK, BLOCK), 0) == lax.broadcasted_iota(jnp.int32, (BLOCK, BLOCK), 1)
    ones = jnp.ones((BLOCK, BLOCK), jnp.bfloat16)
    for buf, (dy, offsets) in zip(camps, LAYOUT):
        for i, dz in enumerate(offsets):
            b = lax.rem(z + dz, NZ) * NY + lax.rem(y + dy, NY)
            tab[b] = buf[i * CBLK : i * CBLK + BLOCK, :]
            row = buf[i * CBLK + BLOCK : (i + 1) * CBLK, :][0:1, 0:BLOCK].astype(jnp.float32)
            diag = jnp.where(eye, jnp.broadcast_to(row, (BLOCK, BLOCK)), 0.0).astype(jnp.bfloat16)
            pb[b] = jnp.dot(diag, ones, preferred_element_type=jnp.float32) * LOG2E
    tab[DEAD] = jnp.zeros((BLOCK, D), jnp.bfloat16)
    pb[DEAD] = jnp.full((BLOCK, BLOCK), -LOWEST, jnp.float32)
    for p in range(TILES * SLOTS):
        tops[p] = jnp.full((8, BLOCK), LOWEST, jnp.float32)
        totals[p] = jnp.zeros((8, BLOCK), jnp.float32)
    for copy in copies:
        copy.wait()
    for q in range(NX * NC):
        stat[q, 2 * TILES :, :] = jnp.concatenate([cost[...], jnp.zeros((4, BLOCK), jnp.float32)], 0)

    def step(i, carry):
        for u in range(UNROLL):
            g = i * UNROLL + u
            slot, t, blocks = unpack(groups[g])
            rows_t = rows[pl.ds(pl.multiple_of(t * BLOCK, BLOCK), BLOCK), :]
            for k in range(2):
                b = blocks[k]
                raw = lax.dot_general(tab[b], rows_t, (((1,), (1,)), ((), ())), preferred_element_type=jnp.float32)
                logit = fold(raw * SCALE2 - pb[b])
                top = jnp.max(logit, axis=0)
                e = jnp.exp2(logit - top[None])
                expo[2 * g + k] = e.reshape(BLOCK, BLOCK)
                tops[slot + k] = top
                totals[slot + k] = jnp.sum(e, axis=0)
        return carry

    lax.fori_loop(0, groups[LAST], step, 0)

    for t in range(TILES):
        top_s = [tops[t * SLOTS + s] for s in range(SLOTS)]
        top8 = functools.reduce(jnp.maximum, top_s)
        top = jnp.max(top8, axis=0, keepdims=True)
        total8 = sum(totals[t * SLOTS + s] * jnp.exp2(top_s[s] - top) for s in range(SLOTS))
        total = jnp.sum(total8, axis=0, keepdims=True)
        for c in range(NX * NC):
            stat[c, t : t + 1, :] = top
            stat[c, TILES + t : TILES + t + 1, :] = total


def spend_kernel(groups, stats, expo, tops, spend, logz, acc, topw):
    owners = NX * NC
    top = functools.reduce(jnp.maximum, [stats[c, 0:TILES, :] for c in range(owners)])
    total = sum(stats[c, TILES : 2 * TILES, :] * jnp.exp2(stats[c, 0:TILES, :] - top) for c in range(owners))
    logz[...] = (top + jnp.log2(total)) * LN2
    topw[0:TILES, :] = top
    cost = jnp.concatenate([stats[c, 2 * TILES : 2 * TILES + 4, :] for c in range(owners)], 0)
    topw[TILES:, :] = cost / total
    for b in range(OWN):
        acc[b] = jnp.zeros((BLOCK, BLOCK), jnp.float32)

    def step(i, carry):
        for u in range(UNROLL):
            g = i * UNROLL + u
            slot, t, blocks = unpack(groups[g])
            top_t = topw[pl.ds(t, 1), :]
            w_t = topw[pl.ds(TILES + t, 1), :]
            for k in range(2):
                factor = jnp.exp2(tops[slot + k] - top_t) * w_t
                b = blocks[k]
                part = fold(expo[2 * g + k]) * factor[None]
                acc[b] = acc[b] + part.reshape(BLOCK, BLOCK)
        return carry

    lax.fori_loop(0, groups[LAST], step, 0)
    for b in range(OWN):
        spend[b : b + 1, :] = jnp.sum(acc[b].T, axis=0, keepdims=True)


VM = pl.BlockSpec(memory_space=pltpu.VMEM)
SM = pl.BlockSpec(memory_space=pltpu.SMEM)
OUT = pltpu.VMEM
GOUT = pltpu.SMEM


def local(imp_emb, imp_cost, camp_emb, prices, spend_limits, block_lists, block_counts):
    imp, camp = lax.axis_index("imp"), lax.axis_index("camp")
    where = jnp.stack([imp // NY, imp % NY, camp // NC, camp % NC]).astype(jnp.int32)

    params = pltpu.CompilerParams(vmem_limit_bytes=VMEM_LIMIT)
    groups = pl.pallas_call(
        prep_kernel,
        in_specs=[SM] * 2,
        out_specs=SM,
        out_shape=GOUT((GROUPS + 1,), jnp.int32),
        name="prep",
    )(block_lists[:, 0, :].T, block_counts[:, 0])

    blk = jnp.concatenate([camp_emb, jnp.pad(prices.reshape(1, BLOCK), ((0, PAD - 1), (0, D - BLOCK)))], 0)
    cost = imp_cost.reshape(4, BLOCK).astype(jnp.float32)
    blk4, plus, minus = shift_z(blk, 4), shift_z(blk, 2), shift_z(blk, -2)
    near = other_core(imp_emb)
    bar = lax.optimization_barrier
    blk4, emb, blk = bar((blk4, imp_emb, blk))
    pair = jnp.concatenate([blk, blk4], 0)
    up, down = shift_z(pair, 1), shift_z(pair, -1)
    b = jnp.concatenate([blk, blk4, plus, minus], 0)
    b_up, b_down = shift_y(b, 1), shift_y(b, -1)
    left, right, across = shift_x(emb, 1), shift_x(emb, -1), shift_x(emb, 2)
    a = jnp.concatenate([up, down], 0)
    a_up, a_down = shift_y(a, 1), shift_y(a, -1)
    b_down, left = bar((b_down, left))
    b_two = shift_y(b_down, -1)
    a_up, left, right, groups, cost = bar((a_up, left, right, groups, cost))
    a_two = shift_y(a_up, 1)
    oleft, oright = other_core(left), other_core(right)
    rows_in = [pltpu.with_memory_space_constraint(imp_emb, pltpu.HBM), left, right, across, near, oleft, oright, other_core(across)]
    camps = [a, b, a_up, a_down, b_up, b_down, a_two, b_two]

    stat, expo, tops = pl.pallas_call(
        stats_kernel,
        in_specs=[SM] * 2 + [pl.BlockSpec(memory_space=pl.ANY)] * 8 + [VM] * 9,
        out_specs=[VM] * 3,
        out_shape=[
            OUT((NX * NC, 2 * TILES + 8, BLOCK), jnp.float32),
            OUT((2 * GROUPS, BLOCK, BLOCK), jnp.float32),
            OUT((TRASH + 2, 8, BLOCK), jnp.float32),
        ],
        scratch_shapes=[
            pltpu.VMEM((TILES * BLOCK, D), jnp.bfloat16),
            pltpu.VMEM((OWN + 1, BLOCK, D), jnp.bfloat16),
            pltpu.VMEM((OWN + 1, BLOCK, BLOCK), jnp.float32),
            pltpu.VMEM((TRASH + 2, 8, BLOCK), jnp.float32),
            pltpu.SemaphoreType.DMA((8,)),
        ],
        compiler_params=params,
        name="stats",
    )(groups, where, *rows_in, *(pltpu.with_memory_space_constraint(v, pltpu.VMEM) for v in camps), cost)

    stats = lax.all_to_all(stat, "camp", 0, 0)

    spend, logz = pl.pallas_call(
        spend_kernel,
        in_specs=[SM] + [VM] * 3,
        out_specs=[VM] * 2,
        out_shape=[
            OUT((OWN, BLOCK), jnp.float32),
            jax.ShapeDtypeStruct((TILES, BLOCK), jnp.float32),
        ],
        scratch_shapes=[
            pltpu.VMEM((OWN + 1, BLOCK, BLOCK), jnp.float32),
            pltpu.VMEM((2 * TILES, BLOCK), jnp.float32),
        ],
        compiler_params=params,
        name="spend",
    )(groups, stats, expo, tops)

    mine = jnp.sum(lax.all_to_all(spend, "imp", 0, 0), axis=0)
    new_prices = prices.astype(jnp.float32) + 2.0 * (mine - spend_limits) / (mine + spend_limits)
    return (new_prices, logz.reshape(TILES * BLOCK))


def solution(mesh):
    return jax.shard_map(
        local,
        mesh=mesh,
        in_specs=(
            P(("imp", "camp"), None),
            P(("imp", "camp")),
            P(("camp", "imp"), None),
            P(("camp", "imp")),
            P(("camp", "imp")),
            P("imp", "camp", None),
            P("imp", "camp"),
        ),
        out_specs=(P(("camp", "imp")), P("imp")),
        check_vma=False,
    )
```

```python
import functools
import math

import jax
import jax.numpy as jnp
from jax import lax
from jax.experimental import pallas as pl
from jax.experimental.pallas import tpu as pltpu
from jax.sharding import PartitionSpec as P

D = 256
BLOCK = 128
SLOTS = 8
NZ, NY, NX, NC = 8, 4, 4, 2
OWN = NZ * NY
TILES = 32
DEAD = OWN
PAD = 16
CBLK = BLOCK + PAD
LOG2E = math.log2(math.e)
LN2 = math.log(2.0)
SCALE2 = 3.0 / math.sqrt(D) * LOG2E
VMEM_LIMIT = 16 * 1024 * 1024
UNROLL = 16
GROUPS = TILES * SLOTS // 2 + UNROLL
LAST = GROUPS
FIRST, SECOND = 1024, 1024 * 64
TRASH = TILES * SLOTS
LOWEST = -3e38


def shift_z(v, k):
    perm = [(z * NY + y, (z + k) % NZ * NY + y) for z in range(NZ) for y in range(NY)]
    return lax.ppermute(v, "imp", perm)


def shift_y(v, k):
    perm = [(z * NY + y, z * NY + (y + k) % NY) for z in range(NZ) for y in range(NY)]
    return lax.ppermute(v, "imp", perm)


def shift_x(v, k):
    perm = [(x * NC + c, (x + k) % NX * NC + c) for x in range(NX) for c in range(NC)]
    return lax.ppermute(v, "camp", perm)


def other_core(v):
    perm = [(x * NC + c, x * NC + 1 - c) for x in range(NX) for c in range(NC)]
    return lax.ppermute(v, "camp", perm)


NEAR, FAR = (7, 3, 1, 5), (0, 4, 6, 2)
LAYOUT = ((0, NEAR), (0, FAR), (3, NEAR), (1, NEAR), (3, FAR), (1, FAR), (2, NEAR), (2, FAR))
DX = (0, 3, 1, 2)


def fold(v):
    return v.reshape(v.shape[0] // 8, 8, v.shape[1])


def prep_kernel(lists, counts, groups):
    def tile(t, at):
        count = counts[t]
        for j in range(SLOTS // 2):
            second = jnp.where(2 * j + 1 < count, lists[2 * j + 1, t], DEAD)
            groups[at] = t * SLOTS + 2 * j + lists[2 * j, t] * FIRST + second * SECOND
            at = at + (2 * j < count).astype(jnp.int32)
        return at

    end = lax.fori_loop(0, TILES, tile, 0)
    for j in range(UNROLL):
        groups[end + j] = TRASH + DEAD * FIRST + DEAD * SECOND
    groups[LAST] = (end + UNROLL - 1) // UNROLL


def unpack(group):
    slot = group & (FIRST - 1)
    return slot, (slot >> 3) & (TILES - 1), ((group >> 10) & 63, group >> 16)


def stats_kernel(groups, where, *refs):
    rows_in, camps, cost = refs[:8], refs[8:16], refs[16]
    stat, expo, tops, rows, tab, pb, totals, sems = refs[17:]
    z, y, x, core = where[0], where[1], where[2], where[3]
    copies = []
    for k in range(8):
        q = lax.rem(x + DX[k % 4], NX) * NC + (core if k < 4 else 1 - core)
        whole = rows.at[pl.ds(pl.multiple_of(q * 512, 512), 512), :]
        copies.append(pltpu.make_async_copy(rows_in[k], whole, sems.at[k]))
    for copy in copies:
        copy.start()
    eye = lax.broadcasted_iota(jnp.int32, (BLOCK, BLOCK), 0) == lax.broadcasted_iota(jnp.int32, (BLOCK, BLOCK), 1)
    ones = jnp.ones((BLOCK, BLOCK), jnp.bfloat16)
    for buf, (dy, offsets) in zip(camps, LAYOUT):
        for i, dz in enumerate(offsets):
            b = lax.rem(z + dz, NZ) * NY + lax.rem(y + dy, NY)
            tab[b] = buf[i * CBLK : i * CBLK + BLOCK, :]
            row = buf[i * CBLK + BLOCK : (i + 1) * CBLK, :][0:1, 0:BLOCK].astype(jnp.float32)
            diag = jnp.where(eye, jnp.broadcast_to(row, (BLOCK, BLOCK)), 0.0).astype(jnp.bfloat16)
            pb[b] = jnp.dot(diag, ones, preferred_element_type=jnp.float32) * LOG2E
    tab[DEAD] = jnp.zeros((BLOCK, D), jnp.bfloat16)
    pb[DEAD] = jnp.full((BLOCK, BLOCK), -LOWEST, jnp.float32)
    for p in range(TILES * SLOTS):
        tops[p] = jnp.full((8, BLOCK), LOWEST, jnp.float32)
        totals[p] = jnp.zeros((8, BLOCK), jnp.float32)
    for copy in copies:
        copy.wait()
    for q in range(NX * NC):
        stat[q, 2 * TILES :, :] = jnp.concatenate([cost[...], jnp.zeros((4, BLOCK), jnp.float32)], 0)

    def step(i, carry):
        for u in range(UNROLL):
            g = i * UNROLL + u
            slot, t, blocks = unpack(groups[g])
            rows_t = rows[pl.ds(pl.multiple_of(t * BLOCK, BLOCK), BLOCK), :]
            for k in range(2):
                b = blocks[k]
                raw = lax.dot_general(tab[b], rows_t, (((1,), (1,)), ((), ())), preferred_element_type=jnp.float32)
                logit = fold(raw * SCALE2 - pb[b])
                top = jnp.max(logit, axis=0)
                e = jnp.exp2(logit - top[None])
                expo[2 * g + k] = e.reshape(BLOCK, BLOCK)
                tops[slot + k] = top
                totals[slot + k] = jnp.sum(e, axis=0)
        return carry

    lax.fori_loop(0, groups[LAST], step, 0)

    for t in range(TILES):
        top_s = [tops[t * SLOTS + s] for s in range(SLOTS)]
        top8 = functools.reduce(jnp.maximum, top_s)
        top = jnp.max(top8, axis=0, keepdims=True)
        total8 = sum(totals[t * SLOTS + s] * jnp.exp2(top_s[s] - top) for s in range(SLOTS))
        total = jnp.sum(total8, axis=0, keepdims=True)
        for c in range(NX * NC):
            stat[c, t : t + 1, :] = top
            stat[c, TILES + t : TILES + t + 1, :] = total


def spend_kernel(groups, stats, expo, tops, spend, logz, acc, topw):
    owners = NX * NC
    top = functools.reduce(jnp.maximum, [stats[c, 0:TILES, :] for c in range(owners)])
    total = sum(stats[c, TILES : 2 * TILES, :] * jnp.exp2(stats[c, 0:TILES, :] - top) for c in range(owners))
    logz[...] = (top + jnp.log2(total)) * LN2
    topw[0:TILES, :] = top
    cost = jnp.concatenate([stats[c, 2 * TILES : 2 * TILES + 4, :] for c in range(owners)], 0)
    topw[TILES:, :] = cost / total
    for b in range(OWN):
        acc[b] = jnp.zeros((BLOCK, BLOCK), jnp.float32)

    def step(i, carry):
        for u in range(UNROLL):
            g = i * UNROLL + u
            slot, t, blocks = unpack(groups[g])
            top_t = topw[pl.ds(t, 1), :]
            w_t = topw[pl.ds(TILES + t, 1), :]
            for k in range(2):
                factor = jnp.exp2(tops[slot + k] - top_t) * w_t
                b = blocks[k]
                part = fold(expo[2 * g + k]) * factor[None]
                acc[b] = acc[b] + part.reshape(BLOCK, BLOCK)
        return carry

    lax.fori_loop(0, groups[LAST], step, 0)
    for b in range(OWN):
        spend[b : b + 1, :] = jnp.sum(acc[b].T, axis=0, keepdims=True)


VM = pl.BlockSpec(memory_space=pltpu.VMEM)
SM = pl.BlockSpec(memory_space=pltpu.SMEM)
OUT = pltpu.VMEM
GOUT = pltpu.SMEM


def local(imp_emb, imp_cost, camp_emb, prices, spend_limits, block_lists, block_counts):
    imp, camp = lax.axis_index("imp"), lax.axis_index("camp")
    where = jnp.stack([imp // NY, imp % NY, camp // NC, camp % NC]).astype(jnp.int32)

    params = pltpu.CompilerParams(vmem_limit_bytes=VMEM_LIMIT)
    groups = pl.pallas_call(
        prep_kernel,
        in_specs=[SM] * 2,
        out_specs=SM,
        out_shape=GOUT((GROUPS + 1,), jnp.int32),
        name="prep",
    )(block_lists[:, 0, :].T, block_counts[:, 0])

    blk = jnp.concatenate([camp_emb, jnp.pad(prices.reshape(1, BLOCK), ((0, PAD - 1), (0, D - BLOCK)))], 0)
    cost = imp_cost.reshape(4, BLOCK).astype(jnp.float32)
    blk4, plus, minus = shift_z(blk, 4), shift_z(blk, 2), shift_z(blk, -2)
    near = other_core(imp_emb)
    bar = lax.optimization_barrier
    blk4, emb, blk = bar((blk4, imp_emb, blk))
    pair = jnp.concatenate([blk, blk4], 0)
    up, down = shift_z(pair, 1), shift_z(pair, -1)
    b = jnp.concatenate([blk, blk4, plus, minus], 0)
    b_up, b_down = shift_y(b, 1), shift_y(b, -1)
    left, right, across = shift_x(emb, 1), shift_x(emb, -1), shift_x(emb, 2)
    a = jnp.concatenate([up, down], 0)
    a_up, a_down = shift_y(a, 1), shift_y(a, -1)
    b_down, left = bar((b_down, left))
    b_two = shift_y(b_down, -1)
    a_up, left, right, groups, cost = bar((a_up, left, right, groups, cost))
    a_two = shift_y(a_up, 1)
    oleft, oright = other_core(left), other_core(right)
    rows_in = [pltpu.with_memory_space_constraint(imp_emb, pltpu.HBM), left, right, across, near, oleft, oright, other_core(across)]
    camps = [a, b, a_up, a_down, b_up, b_down, a_two, b_two]

    stat, expo, tops = pl.pallas_call(
        stats_kernel,
        in_specs=[SM] * 2 + [pl.BlockSpec(memory_space=pl.ANY)] * 8 + [VM] * 9,
        out_specs=[VM] * 3,
        out_shape=[
            OUT((NX * NC, 2 * TILES + 8, BLOCK), jnp.float32),
            OUT((2 * GROUPS, BLOCK, BLOCK), jnp.float32),
            OUT((TRASH + 2, 8, BLOCK), jnp.float32),
        ],
        scratch_shapes=[
            pltpu.VMEM((TILES * BLOCK, D), jnp.bfloat16),
            pltpu.VMEM((OWN + 1, BLOCK, D), jnp.bfloat16),
            pltpu.VMEM((OWN + 1, BLOCK, BLOCK), jnp.float32),
            pltpu.VMEM((TRASH + 2, 8, BLOCK), jnp.float32),
            pltpu.SemaphoreType.DMA((8,)),
        ],
        compiler_params=params,
        name="stats",
    )(groups, where, *rows_in, *(pltpu.with_memory_space_constraint(v, pltpu.VMEM) for v in camps), cost)

    stats = lax.all_to_all(stat, "camp", 0, 0)

    spend, logz = pl.pallas_call(
        spend_kernel,
        in_specs=[SM] + [VM] * 3,
        out_specs=[VM] * 2,
        out_shape=[
            OUT((OWN, BLOCK), jnp.float32),
            jax.ShapeDtypeStruct((TILES, BLOCK), jnp.float32),
        ],
        scratch_shapes=[
            pltpu.VMEM((OWN + 1, BLOCK, BLOCK), jnp.float32),
            pltpu.VMEM((2 * TILES, BLOCK), jnp.float32),
        ],
        compiler_params=params,
        name="spend",
    )(groups, stats, expo, tops)

    mine = jnp.sum(lax.all_to_all(spend, "imp", 0, 0), axis=0)
    new_prices = prices.astype(jnp.float32) + 2.0 * (mine - spend_limits) / (mine + spend_limits)
    return (new_prices, logz.reshape(TILES * BLOCK))


def solution(mesh):
    return jax.shard_map(
        local,
        mesh=mesh,
        in_specs=(
            P(("imp", "camp"), None),
            P(("imp", "camp")),
            P(("camp", "imp"), None),
            P(("camp", "imp")),
            P(("camp", "imp")),
            P("imp", "camp", None),
            P("imp", "camp"),
        ),
        out_specs=(P(("camp", "imp")), P("imp")),
        check_vma=False,
    )
```

```python
import functools
import math

import jax
import jax.numpy as jnp
from jax import lax
from jax.experimental import pallas as pl
from jax.experimental.pallas import tpu as pltpu
from jax.sharding import PartitionSpec as P

D = 256
BLOCK = 128
SLOTS = 8
NZ, NY, NX, NC = 8, 4, 4, 2
OWN = NZ * NY
TILES = 32
DEAD = OWN
PAD = 16
CBLK = BLOCK + PAD
LOG2E = math.log2(math.e)
LN2 = math.log(2.0)
SCALE2 = 3.0 / math.sqrt(D) * LOG2E
VMEM_LIMIT = 16 * 1024 * 1024
UNROLL = 16
GROUPS = TILES * SLOTS // 2 + UNROLL
LAST = GROUPS
FIRST, SECOND = 1024, 1024 * 64
TRASH = TILES * SLOTS
LOWEST = -3e38


def shift_z(v, k):
    perm = [(z * NY + y, (z + k) % NZ * NY + y) for z in range(NZ) for y in range(NY)]
    return lax.ppermute(v, "imp", perm)


def shift_y(v, k):
    perm = [(z * NY + y, z * NY + (y + k) % NY) for z in range(NZ) for y in range(NY)]
    return lax.ppermute(v, "imp", perm)


def shift_x(v, k):
    perm = [(x * NC + c, (x + k) % NX * NC + c) for x in range(NX) for c in range(NC)]
    return lax.ppermute(v, "camp", perm)


def other_core(v):
    perm = [(x * NC + c, x * NC + 1 - c) for x in range(NX) for c in range(NC)]
    return lax.ppermute(v, "camp", perm)


NEAR, FAR = (7, 3, 1, 5), (0, 4, 6, 2)
LAYOUT = ((0, NEAR), (0, FAR), (3, NEAR), (1, NEAR), (3, FAR), (1, FAR), (2, NEAR), (2, FAR))
DX = (0, 3, 1, 2)


def fold(v):
    return v.reshape(v.shape[0] // 8, 8, v.shape[1])


def prep_kernel(lists, counts, groups):
    def tile(t, at):
        count = counts[t]
        for j in range(SLOTS // 2):
            second = jnp.where(2 * j + 1 < count, lists[2 * j + 1, t], DEAD)
            groups[at] = t * SLOTS + 2 * j + lists[2 * j, t] * FIRST + second * SECOND
            at = at + (2 * j < count).astype(jnp.int32)
        return at

    end = lax.fori_loop(0, TILES, tile, 0)
    for j in range(UNROLL):
        groups[end + j] = TRASH + DEAD * FIRST + DEAD * SECOND
    groups[LAST] = (end + UNROLL - 1) // UNROLL


def unpack(group):
    slot = group & (FIRST - 1)
    return slot, (slot >> 3) & (TILES - 1), ((group >> 10) & 63, group >> 16)


def stats_kernel(groups, where, *refs):
    rows_in, camps, cost = refs[:8], refs[8:16], refs[16]
    stat, expo, tops, rows, tab, pb, totals, sems = refs[17:]
    z, y, x, core = where[0], where[1], where[2], where[3]
    copies = []
    for k in range(8):
        q = lax.rem(x + DX[k % 4], NX) * NC + (core if k < 4 else 1 - core)
        whole = rows.at[pl.ds(pl.multiple_of(q * 512, 512), 512), :]
        copies.append(pltpu.make_async_copy(rows_in[k], whole, sems.at[k]))
    for copy in copies:
        copy.start()
    eye = lax.broadcasted_iota(jnp.int32, (BLOCK, BLOCK), 0) == lax.broadcasted_iota(jnp.int32, (BLOCK, BLOCK), 1)
    ones = jnp.ones((BLOCK, BLOCK), jnp.bfloat16)
    for buf, (dy, offsets) in zip(camps, LAYOUT):
        for i, dz in enumerate(offsets):
            b = lax.rem(z + dz, NZ) * NY + lax.rem(y + dy, NY)
            tab[b] = buf[i * CBLK : i * CBLK + BLOCK, :]
            row = buf[i * CBLK + BLOCK : (i + 1) * CBLK, :][0:1, 0:BLOCK].astype(jnp.float32)
            diag = jnp.where(eye, jnp.broadcast_to(row, (BLOCK, BLOCK)), 0.0).astype(jnp.bfloat16)
            pb[b] = jnp.dot(diag, ones, preferred_element_type=jnp.float32) * LOG2E
    tab[DEAD] = jnp.zeros((BLOCK, D), jnp.bfloat16)
    pb[DEAD] = jnp.full((BLOCK, BLOCK), -LOWEST, jnp.float32)
    for p in range(TILES * SLOTS):
        tops[p] = jnp.full((8, BLOCK), LOWEST, jnp.float32)
        totals[p] = jnp.zeros((8, BLOCK), jnp.float32)
    for copy in copies:
        copy.wait()
    for q in range(NX * NC):
        stat[q, 2 * TILES :, :] = jnp.concatenate([cost[...], jnp.zeros((4, BLOCK), jnp.float32)], 0)

    def step(i, carry):
        for u in range(UNROLL):
            g = i * UNROLL + u
            slot, t, blocks = unpack(groups[g])
            rows_t = rows[pl.ds(pl.multiple_of(t * BLOCK, BLOCK), BLOCK), :]
            for k in range(2):
                b = blocks[k]
                raw = lax.dot_general(tab[b], rows_t, (((1,), (1,)), ((), ())), preferred_element_type=jnp.float32)
                logit = fold(raw * SCALE2 - pb[b])
                top = jnp.max(logit, axis=0)
                e = jnp.exp2(logit - top[None])
                expo[2 * g + k] = e.reshape(BLOCK, BLOCK)
                tops[slot + k] = top
                totals[slot + k] = jnp.sum(e, axis=0)
        return carry

    lax.fori_loop(0, groups[LAST], step, 0)

    for t in range(TILES):
        top_s = [tops[t * SLOTS + s] for s in range(SLOTS)]
        top8 = functools.reduce(jnp.maximum, top_s)
        top = jnp.max(top8, axis=0, keepdims=True)
        total8 = sum(totals[t * SLOTS + s] * jnp.exp2(top_s[s] - top) for s in range(SLOTS))
        total = jnp.sum(total8, axis=0, keepdims=True)
        for c in range(NX * NC):
            stat[c, t : t + 1, :] = top
            stat[c, TILES + t : TILES + t + 1, :] = total


def spend_kernel(groups, stats, expo, tops, spend, logz, acc, topw):
    owners = NX * NC
    top = functools.reduce(jnp.maximum, [stats[c, 0:TILES, :] for c in range(owners)])
    total = sum(stats[c, TILES : 2 * TILES, :] * jnp.exp2(stats[c, 0:TILES, :] - top) for c in range(owners))
    logz[...] = (top + jnp.log2(total)) * LN2
    topw[0:TILES, :] = top
    cost = jnp.concatenate([stats[c, 2 * TILES : 2 * TILES + 4, :] for c in range(owners)], 0)
    topw[TILES:, :] = cost / total
    for b in range(OWN):
        acc[b] = jnp.zeros((BLOCK, BLOCK), jnp.float32)

    def step(i, carry):
        for u in range(UNROLL):
            g = i * UNROLL + u
            slot, t, blocks = unpack(groups[g])
            top_t = topw[pl.ds(t, 1), :]
            w_t = topw[pl.ds(TILES + t, 1), :]
            for k in range(2):
                factor = jnp.exp2(tops[slot + k] - top_t) * w_t
                b = blocks[k]
                part = fold(expo[2 * g + k]) * factor[None]
                acc[b] = acc[b] + part.reshape(BLOCK, BLOCK)
        return carry

    lax.fori_loop(0, groups[LAST], step, 0)
    for b in range(OWN):
        spend[b : b + 1, :] = jnp.sum(acc[b].T, axis=0, keepdims=True)


VM = pl.BlockSpec(memory_space=pltpu.VMEM)
SM = pl.BlockSpec(memory_space=pltpu.SMEM)
OUT = pltpu.VMEM
GOUT = pltpu.SMEM


def local(imp_emb, imp_cost, camp_emb, prices, spend_limits, block_lists, block_counts):
    imp, camp = lax.axis_index("imp"), lax.axis_index("camp")
    where = jnp.stack([imp // NY, imp % NY, camp // NC, camp % NC]).astype(jnp.int32)

    params = pltpu.CompilerParams(vmem_limit_bytes=VMEM_LIMIT)
    groups = pl.pallas_call(
        prep_kernel,
        in_specs=[SM] * 2,
        out_specs=SM,
        out_shape=GOUT((GROUPS + 1,), jnp.int32),
        name="prep",
    )(block_lists[:, 0, :].T, block_counts[:, 0])

    blk = jnp.concatenate([camp_emb, jnp.pad(prices.reshape(1, BLOCK), ((0, PAD - 1), (0, D - BLOCK)))], 0)
    cost = imp_cost.reshape(4, BLOCK).astype(jnp.float32)
    blk4, plus, minus = shift_z(blk, 4), shift_z(blk, 2), shift_z(blk, -2)
    near = other_core(imp_emb)
    bar = lax.optimization_barrier
    blk4, blk = bar((blk4, blk))
    pair = jnp.concatenate([blk, blk4], 0)
    up, down = shift_z(pair, 1), shift_z(pair, -1)
    b = jnp.concatenate([blk, blk4, plus, minus], 0)
    b_up, b_down = shift_y(b, 1), shift_y(b, -1)
    left, right, across = shift_x(imp_emb, 1), shift_x(imp_emb, -1), shift_x(imp_emb, 2)
    a = jnp.concatenate([up, down], 0)
    a_up, a_down = shift_y(a, 1), shift_y(a, -1)
    b_down, left = bar((b_down, left))
    b_two = shift_y(b_down, -1)
    a_up, left, right, groups, cost = bar((a_up, left, right, groups, cost))
    a_two = shift_y(a_up, 1)
    oleft, oright = other_core(left), other_core(right)
    rows_in = [pltpu.with_memory_space_constraint(imp_emb, pltpu.HBM), left, right, across, near, oleft, oright, other_core(across)]
    camps = [a, b, a_up, a_down, b_up, b_down, a_two, b_two]

    stat, expo, tops = pl.pallas_call(
        stats_kernel,
        in_specs=[SM] * 2 + [pl.BlockSpec(memory_space=pl.ANY)] * 8 + [VM] * 9,
        out_specs=[VM] * 3,
        out_shape=[
            OUT((NX * NC, 2 * TILES + 8, BLOCK), jnp.float32),
            OUT((2 * GROUPS, BLOCK, BLOCK), jnp.float32),
            OUT((TRASH + 2, 8, BLOCK), jnp.float32),
        ],
        scratch_shapes=[
            pltpu.VMEM((TILES * BLOCK, D), jnp.bfloat16),
            pltpu.VMEM((OWN + 1, BLOCK, D), jnp.bfloat16),
            pltpu.VMEM((OWN + 1, BLOCK, BLOCK), jnp.float32),
            pltpu.VMEM((TRASH + 2, 8, BLOCK), jnp.float32),
            pltpu.SemaphoreType.DMA((8,)),
        ],
        compiler_params=params,
        name="stats",
    )(groups, where, *rows_in, *(pltpu.with_memory_space_constraint(v, pltpu.VMEM) for v in camps), cost)

    stats = lax.all_to_all(stat, "camp", 0, 0)

    spend, logz = pl.pallas_call(
        spend_kernel,
        in_specs=[SM] + [VM] * 3,
        out_specs=[VM] * 2,
        out_shape=[
            OUT((OWN, BLOCK), jnp.float32),
            jax.ShapeDtypeStruct((TILES, BLOCK), jnp.float32),
        ],
        scratch_shapes=[
            pltpu.VMEM((OWN + 1, BLOCK, BLOCK), jnp.float32),
            pltpu.VMEM((2 * TILES, BLOCK), jnp.float32),
        ],
        compiler_params=params,
        name="spend",
    )(groups, stats, expo, tops)

    mine = jnp.sum(lax.all_to_all(spend, "imp", 0, 0), axis=0)
    new_prices = prices.astype(jnp.float32) + 2.0 * (mine - spend_limits) / (mine + spend_limits)
    return (new_prices, logz.reshape(TILES * BLOCK))


def solution(mesh):
    return jax.shard_map(
        local,
        mesh=mesh,
        in_specs=(
            P(("imp", "camp"), None),
            P(("imp", "camp")),
            P(("camp", "imp"), None),
            P(("camp", "imp")),
            P(("camp", "imp")),
            P("imp", "camp", None),
            P("imp", "camp"),
        ),
        out_specs=(P(("camp", "imp")), P("imp")),
        check_vma=False,
    )
```

```python
import functools
import math

import jax
import jax.numpy as jnp
from jax import lax
from jax.experimental import pallas as pl
from jax.experimental.pallas import tpu as pltpu
from jax.sharding import PartitionSpec as P

D = 256
BLOCK = 128
SLOTS = 8
NZ, NY, NX, NC = 8, 4, 4, 2
OWN = NZ * NY
TILES = 32
DEAD = OWN
PAD = 16
CBLK = BLOCK + PAD
LOG2E = math.log2(math.e)
LN2 = math.log(2.0)
SCALE2 = 3.0 / math.sqrt(D) * LOG2E
VMEM_LIMIT = 16 * 1024 * 1024
UNROLL = 16
GROUPS = TILES * SLOTS // 2 + UNROLL
LAST = GROUPS
FIRST, SECOND = 1024, 1024 * 64
TRASH = TILES * SLOTS
LOWEST = -3e38


def shift_z(v, k):
    perm = [(z * NY + y, (z + k) % NZ * NY + y) for z in range(NZ) for y in range(NY)]
    return lax.ppermute(v, "imp", perm)


def shift_y(v, k):
    perm = [(z * NY + y, z * NY + (y + k) % NY) for z in range(NZ) for y in range(NY)]
    return lax.ppermute(v, "imp", perm)


def shift_x(v, k):
    perm = [(x * NC + c, (x + k) % NX * NC + c) for x in range(NX) for c in range(NC)]
    return lax.ppermute(v, "camp", perm)


def other_core(v):
    perm = [(x * NC + c, x * NC + 1 - c) for x in range(NX) for c in range(NC)]
    return lax.ppermute(v, "camp", perm)


NEAR, FAR = (7, 3, 1, 5), (0, 4, 6, 2)
LAYOUT = ((0, NEAR), (0, FAR), (3, NEAR), (1, NEAR), (3, FAR), (1, FAR), (2, NEAR), (2, FAR))
DX = (0, 3, 1, 2)


def fold(v):
    return v.reshape(v.shape[0] // 8, 8, v.shape[1])


def prep_kernel(lists, counts, groups):
    def tile(t, at):
        count = counts[t]
        for j in range(SLOTS // 2):
            second = jnp.where(2 * j + 1 < count, lists[2 * j + 1, t], DEAD)
            groups[at] = t * SLOTS + 2 * j + lists[2 * j, t] * FIRST + second * SECOND
            at = at + (2 * j < count).astype(jnp.int32)
        return at

    end = lax.fori_loop(0, TILES, tile, 0)
    for j in range(UNROLL):
        groups[end + j] = TRASH + DEAD * FIRST + DEAD * SECOND
    groups[LAST] = (end + UNROLL - 1) // UNROLL


def unpack(group):
    slot = group & (FIRST - 1)
    return slot, (slot >> 3) & (TILES - 1), ((group >> 10) & 63, group >> 16)


def stats_kernel(groups, where, *refs):
    rows_in, camps, cost = refs[:8], refs[8:16], refs[16]
    stat, expo, tops, rows, tab, pb, totals, sems = refs[17:]
    z, y, x, core = where[0], where[1], where[2], where[3]
    copies = []
    for k in range(8):
        q = lax.rem(x + DX[k % 4], NX) * NC + (core if k < 4 else 1 - core)
        whole = rows.at[pl.ds(pl.multiple_of(q * 512, 512), 512), :]
        copies.append(pltpu.make_async_copy(rows_in[k], whole, sems.at[k]))
    for copy in copies:
        copy.start()
    eye = lax.broadcasted_iota(jnp.int32, (BLOCK, BLOCK), 0) == lax.broadcasted_iota(jnp.int32, (BLOCK, BLOCK), 1)
    ones = jnp.ones((BLOCK, BLOCK), jnp.bfloat16)
    for buf, (dy, offsets) in zip(camps, LAYOUT):
        for i, dz in enumerate(offsets):
            b = lax.rem(z + dz, NZ) * NY + lax.rem(y + dy, NY)
            tab[b] = buf[i * CBLK : i * CBLK + BLOCK, :]
            row = buf[i * CBLK + BLOCK : (i + 1) * CBLK, :][0:1, 0:BLOCK].astype(jnp.float32)
            diag = jnp.where(eye, jnp.broadcast_to(row, (BLOCK, BLOCK)), 0.0).astype(jnp.bfloat16)
            pb[b] = jnp.dot(diag, ones, preferred_element_type=jnp.float32) * LOG2E
    tab[DEAD] = jnp.zeros((BLOCK, D), jnp.bfloat16)
    pb[DEAD] = jnp.full((BLOCK, BLOCK), -LOWEST, jnp.float32)
    for p in range(TILES * SLOTS):
        tops[p] = jnp.full((8, BLOCK), LOWEST, jnp.float32)
        totals[p] = jnp.zeros((8, BLOCK), jnp.float32)
    for copy in copies:
        copy.wait()
    for q in range(NX * NC):
        stat[q, 2 * TILES :, :] = jnp.concatenate([cost[...], jnp.zeros((4, BLOCK), jnp.float32)], 0)

    def step(i, carry):
        for u in range(UNROLL):
            g = i * UNROLL + u
            slot, t, blocks = unpack(groups[g])
            rows_t = rows[pl.ds(pl.multiple_of(t * BLOCK, BLOCK), BLOCK), :]
            for k in range(2):
                b = blocks[k]
                raw = lax.dot_general(tab[b], rows_t, (((1,), (1,)), ((), ())), preferred_element_type=jnp.float32)
                logit = fold(raw * SCALE2 - pb[b])
                top = jnp.max(logit, axis=0)
                e = jnp.exp2(logit - top[None])
                expo[2 * g + k] = e.reshape(BLOCK, BLOCK)
                tops[slot + k] = top
                totals[slot + k] = jnp.sum(e, axis=0)
        return carry

    lax.fori_loop(0, groups[LAST], step, 0)

    for t in range(TILES):
        top_s = [tops[t * SLOTS + s] for s in range(SLOTS)]
        top8 = functools.reduce(jnp.maximum, top_s)
        top = jnp.max(top8, axis=0, keepdims=True)
        total8 = sum(totals[t * SLOTS + s] * jnp.exp2(top_s[s] - top) for s in range(SLOTS))
        total = jnp.sum(total8, axis=0, keepdims=True)
        stat[0, t : t + 1, :] = top
        stat[0, TILES + t : TILES + t + 1, :] = total
    block = stat[0, 0 : 2 * TILES, :]
    for c in range(1, NX * NC):
        stat[c, 0 : 2 * TILES, :] = block


def spend_kernel(groups, stats, expo, tops, spend, logz, acc, topw):
    owners = NX * NC
    top = functools.reduce(jnp.maximum, [stats[c, 0:TILES, :] for c in range(owners)])
    total = sum(stats[c, TILES : 2 * TILES, :] * jnp.exp2(stats[c, 0:TILES, :] - top) for c in range(owners))
    logz[...] = (top + jnp.log2(total)) * LN2
    topw[0:TILES, :] = top
    cost = jnp.concatenate([stats[c, 2 * TILES : 2 * TILES + 4, :] for c in range(owners)], 0)
    topw[TILES:, :] = cost / total
    for b in range(OWN):
        acc[b] = jnp.zeros((BLOCK, BLOCK), jnp.float32)

    def step(i, carry):
        for u in range(UNROLL):
            g = i * UNROLL + u
            slot, t, blocks = unpack(groups[g])
            top_t = topw[pl.ds(t, 1), :]
            w_t = topw[pl.ds(TILES + t, 1), :]
            for k in range(2):
                factor = jnp.exp2(tops[slot + k] - top_t) * w_t
                b = blocks[k]
                part = fold(expo[2 * g + k]) * factor[None]
                acc[b] = acc[b] + part.reshape(BLOCK, BLOCK)
        return carry

    lax.fori_loop(0, groups[LAST], step, 0)
    for b in range(OWN):
        spend[b : b + 1, :] = jnp.sum(acc[b].T, axis=0, keepdims=True)


VM = pl.BlockSpec(memory_space=pltpu.VMEM)
SM = pl.BlockSpec(memory_space=pltpu.SMEM)
OUT = pltpu.VMEM
GOUT = pltpu.SMEM


def local(imp_emb, imp_cost, camp_emb, prices, spend_limits, block_lists, block_counts):
    imp, camp = lax.axis_index("imp"), lax.axis_index("camp")
    where = jnp.stack([imp // NY, imp % NY, camp // NC, camp % NC]).astype(jnp.int32)

    params = pltpu.CompilerParams(vmem_limit_bytes=VMEM_LIMIT)
    groups = pl.pallas_call(
        prep_kernel,
        in_specs=[SM] * 2,
        out_specs=SM,
        out_shape=GOUT((GROUPS + 1,), jnp.int32),
        name="prep",
    )(block_lists[:, 0, :].T, block_counts[:, 0])

    blk = jnp.concatenate([camp_emb, jnp.pad(prices.reshape(1, BLOCK), ((0, PAD - 1), (0, D - BLOCK)))], 0)
    cost = imp_cost.reshape(4, BLOCK).astype(jnp.float32)
    blk4, plus, minus = shift_z(blk, 4), shift_z(blk, 2), shift_z(blk, -2)
    near = other_core(imp_emb)
    bar = lax.optimization_barrier
    blk4, blk = bar((blk4, blk))
    pair = jnp.concatenate([blk, blk4], 0)
    up, down = shift_z(pair, 1), shift_z(pair, -1)
    b = jnp.concatenate([blk, blk4, plus, minus], 0)
    b_up, b_down = shift_y(b, 1), shift_y(b, -1)
    left, right, across = shift_x(imp_emb, 1), shift_x(imp_emb, -1), shift_x(imp_emb, 2)
    a = jnp.concatenate([up, down], 0)
    a_up, a_down = shift_y(a, 1), shift_y(a, -1)
    b_down, left = bar((b_down, left))
    b_two = shift_y(b_down, -1)
    a_up, left, right, groups, cost = bar((a_up, left, right, groups, cost))
    a_two = shift_y(a_up, 1)
    oleft, oright = other_core(left), other_core(right)
    rows_in = [pltpu.with_memory_space_constraint(imp_emb, pltpu.HBM), left, right, across, near, oleft, oright, other_core(across)]
    camps = [a, b, a_up, a_down, b_up, b_down, a_two, b_two]

    stat, expo, tops = pl.pallas_call(
        stats_kernel,
        in_specs=[SM] * 2 + [pl.BlockSpec(memory_space=pl.ANY)] * 8 + [VM] * 9,
        out_specs=[VM] * 3,
        out_shape=[
            OUT((NX * NC, 2 * TILES + 8, BLOCK), jnp.float32),
            OUT((2 * GROUPS, BLOCK, BLOCK), jnp.float32),
            OUT((TRASH + 2, 8, BLOCK), jnp.float32),
        ],
        scratch_shapes=[
            pltpu.VMEM((TILES * BLOCK, D), jnp.bfloat16),
            pltpu.VMEM((OWN + 1, BLOCK, D), jnp.bfloat16),
            pltpu.VMEM((OWN + 1, BLOCK, BLOCK), jnp.float32),
            pltpu.VMEM((TRASH + 2, 8, BLOCK), jnp.float32),
            pltpu.SemaphoreType.DMA((8,)),
        ],
        compiler_params=params,
        name="stats",
    )(groups, where, *rows_in, *(pltpu.with_memory_space_constraint(v, pltpu.VMEM) for v in camps), cost)

    stats = lax.all_to_all(stat, "camp", 0, 0)

    spend, logz = pl.pallas_call(
        spend_kernel,
        in_specs=[SM] + [VM] * 3,
        out_specs=[VM] * 2,
        out_shape=[
            OUT((OWN, BLOCK), jnp.float32),
            jax.ShapeDtypeStruct((TILES, BLOCK), jnp.float32),
        ],
        scratch_shapes=[
            pltpu.VMEM((OWN + 1, BLOCK, BLOCK), jnp.float32),
            pltpu.VMEM((2 * TILES, BLOCK), jnp.float32),
        ],
        compiler_params=params,
        name="spend",
    )(groups, stats, expo, tops)

    mine = jnp.sum(lax.all_to_all(spend, "imp", 0, 0), axis=0)
    new_prices = prices.astype(jnp.float32) + 2.0 * (mine - spend_limits) / (mine + spend_limits)
    return (new_prices, logz.reshape(TILES * BLOCK))


def solution(mesh):
    return jax.shard_map(
        local,
        mesh=mesh,
        in_specs=(
            P(("imp", "camp"), None),
            P(("imp", "camp")),
            P(("camp", "imp"), None),
            P(("camp", "imp")),
            P(("camp", "imp")),
            P("imp", "camp", None),
            P("imp", "camp"),
        ),
        out_specs=(P(("camp", "imp")), P("imp")),
        check_vma=False,
    )
```

```python
import functools
import math

import jax
import jax.numpy as jnp
from jax import lax
from jax.experimental import pallas as pl
from jax.experimental.pallas import tpu as pltpu
from jax.sharding import PartitionSpec as P

D = 256
BLOCK = 128
SLOTS = 8
NZ, NY, NX, NC = 8, 4, 4, 2
OWN = NZ * NY
TILES = 32
DEAD = OWN
PAD = 16
CBLK = BLOCK + PAD
LOG2E = math.log2(math.e)
LN2 = math.log(2.0)
SCALE2 = 3.0 / math.sqrt(D) * LOG2E
VMEM_LIMIT = 16 * 1024 * 1024
UNROLL = 20
GROUPS = TILES * SLOTS // 2 + UNROLL
LAST = GROUPS
FIRST, SECOND = 1024, 1024 * 64
TRASH = TILES * SLOTS
LOWEST = -3e38


def shift_z(v, k):
    perm = [(z * NY + y, (z + k) % NZ * NY + y) for z in range(NZ) for y in range(NY)]
    return lax.ppermute(v, "imp", perm)


def shift_y(v, k):
    perm = [(z * NY + y, z * NY + (y + k) % NY) for z in range(NZ) for y in range(NY)]
    return lax.ppermute(v, "imp", perm)


def shift_x(v, k):
    perm = [(x * NC + c, (x + k) % NX * NC + c) for x in range(NX) for c in range(NC)]
    return lax.ppermute(v, "camp", perm)


def other_core(v):
    perm = [(x * NC + c, x * NC + 1 - c) for x in range(NX) for c in range(NC)]
    return lax.ppermute(v, "camp", perm)


NEAR, FAR = (7, 3, 1, 5), (0, 4, 6, 2)
LAYOUT = ((0, NEAR), (0, FAR), (3, NEAR), (1, NEAR), (3, FAR), (1, FAR), (2, NEAR), (2, FAR))
DX = (0, 3, 1, 2)


def fold(v):
    return v.reshape(v.shape[0] // 8, 8, v.shape[1])


def prep_kernel(lists, counts, groups):
    def tile(t, at):
        count = counts[t]
        for j in range(SLOTS // 2):
            second = jnp.where(2 * j + 1 < count, lists[2 * j + 1, t], DEAD)
            groups[at] = t * SLOTS + 2 * j + lists[2 * j, t] * FIRST + second * SECOND
            at = at + (2 * j < count).astype(jnp.int32)
        return at

    end = lax.fori_loop(0, TILES, tile, 0)
    for j in range(UNROLL):
        groups[end + j] = TRASH + DEAD * FIRST + DEAD * SECOND
    groups[LAST] = (end + UNROLL - 1) // UNROLL


def unpack(group):
    slot = group & (FIRST - 1)
    return slot, (slot >> 3) & (TILES - 1), ((group >> 10) & 63, group >> 16)


def stats_kernel(groups, where, *refs):
    rows_in, camps, cost = refs[:8], refs[8:16], refs[16]
    stat, expo, tops, rows, tab, pb, totals, sems = refs[17:]
    z, y, x, core = where[0], where[1], where[2], where[3]
    copies = []
    for k in range(8):
        q = lax.rem(x + DX[k % 4], NX) * NC + (core if k < 4 else 1 - core)
        whole = rows.at[pl.ds(pl.multiple_of(q * 512, 512), 512), :]
        copies.append(pltpu.make_async_copy(rows_in[k], whole, sems.at[k]))
    for copy in copies:
        copy.start()
    eye = lax.broadcasted_iota(jnp.int32, (BLOCK, BLOCK), 0) == lax.broadcasted_iota(jnp.int32, (BLOCK, BLOCK), 1)
    ones = jnp.ones((BLOCK, BLOCK), jnp.bfloat16)
    for buf, (dy, offsets) in zip(camps, LAYOUT):
        for i, dz in enumerate(offsets):
            b = lax.rem(z + dz, NZ) * NY + lax.rem(y + dy, NY)
            tab[b] = buf[i * CBLK : i * CBLK + BLOCK, :]
            row = buf[i * CBLK + BLOCK : (i + 1) * CBLK, :][0:1, 0:BLOCK].astype(jnp.float32)
            diag = jnp.where(eye, jnp.broadcast_to(row, (BLOCK, BLOCK)), 0.0).astype(jnp.bfloat16)
            pb[b] = jnp.dot(diag, ones, preferred_element_type=jnp.float32) * LOG2E
    tab[DEAD] = jnp.zeros((BLOCK, D), jnp.bfloat16)
    pb[DEAD] = jnp.full((BLOCK, BLOCK), -LOWEST, jnp.float32)
    for p in range(TILES * SLOTS):
        tops[p] = jnp.full((8, BLOCK), LOWEST, jnp.float32)
        totals[p] = jnp.zeros((8, BLOCK), jnp.float32)
    for copy in copies:
        copy.wait()
    for q in range(NX * NC):
        stat[q, 2 * TILES :, :] = jnp.concatenate([cost[...], jnp.zeros((4, BLOCK), jnp.float32)], 0)

    def step(i, carry):
        for u in range(UNROLL):
            g = i * UNROLL + u
            slot, t, blocks = unpack(groups[g])
            rows_t = rows[pl.ds(pl.multiple_of(t * BLOCK, BLOCK), BLOCK), :]
            for k in range(2):
                b = blocks[k]
                raw = lax.dot_general(tab[b], rows_t, (((1,), (1,)), ((), ())), preferred_element_type=jnp.float32)
                logit = fold(raw * SCALE2 - pb[b])
                top = jnp.max(logit, axis=0)
                e = jnp.exp2(logit - top[None])
                expo[2 * g + k] = e.reshape(BLOCK, BLOCK)
                tops[slot + k] = top
                totals[slot + k] = jnp.sum(e, axis=0)
        return carry

    lax.fori_loop(0, groups[LAST], step, 0)

    for t in range(TILES):
        top_s = [tops[t * SLOTS + s] for s in range(SLOTS)]
        top8 = functools.reduce(jnp.maximum, top_s)
        top = jnp.max(top8, axis=0, keepdims=True)
        total8 = sum(totals[t * SLOTS + s] * jnp.exp2(top_s[s] - top) for s in range(SLOTS))
        total = jnp.sum(total8, axis=0, keepdims=True)
        for c in range(NX * NC):
            stat[c, t : t + 1, :] = top
            stat[c, TILES + t : TILES + t + 1, :] = total


def spend_kernel(groups, stats, expo, tops, spend, logz, acc, topw):
    owners = NX * NC
    top = functools.reduce(jnp.maximum, [stats[c, 0:TILES, :] for c in range(owners)])
    total = sum(stats[c, TILES : 2 * TILES, :] * jnp.exp2(stats[c, 0:TILES, :] - top) for c in range(owners))
    logz[...] = (top + jnp.log2(total)) * LN2
    topw[0:TILES, :] = top
    cost = jnp.concatenate([stats[c, 2 * TILES : 2 * TILES + 4, :] for c in range(owners)], 0)
    topw[TILES:, :] = cost / total
    for b in range(OWN):
        acc[b] = jnp.zeros((BLOCK, BLOCK), jnp.float32)

    def step(i, carry):
        for u in range(UNROLL):
            g = i * UNROLL + u
            slot, t, blocks = unpack(groups[g])
            top_t = topw[pl.ds(t, 1), :]
            w_t = topw[pl.ds(TILES + t, 1), :]
            for k in range(2):
                factor = jnp.exp2(tops[slot + k] - top_t) * w_t
                b = blocks[k]
                part = fold(expo[2 * g + k]) * factor[None]
                acc[b] = acc[b] + part.reshape(BLOCK, BLOCK)
        return carry

    lax.fori_loop(0, groups[LAST], step, 0)
    for b in range(OWN):
        spend[b : b + 1, :] = jnp.sum(acc[b].T, axis=0, keepdims=True)


VM = pl.BlockSpec(memory_space=pltpu.VMEM)
SM = pl.BlockSpec(memory_space=pltpu.SMEM)
OUT = pltpu.VMEM
GOUT = pltpu.SMEM


def local(imp_emb, imp_cost, camp_emb, prices, spend_limits, block_lists, block_counts):
    imp, camp = lax.axis_index("imp"), lax.axis_index("camp")
    where = jnp.stack([imp // NY, imp % NY, camp // NC, camp % NC]).astype(jnp.int32)

    params = pltpu.CompilerParams(vmem_limit_bytes=VMEM_LIMIT)
    groups = pl.pallas_call(
        prep_kernel,
        in_specs=[SM] * 2,
        out_specs=SM,
        out_shape=GOUT((GROUPS + 1,), jnp.int32),
        name="prep",
    )(block_lists[:, 0, :].T, block_counts[:, 0])

    blk = jnp.concatenate([camp_emb, jnp.pad(prices.reshape(1, BLOCK), ((0, PAD - 1), (0, D - BLOCK)))], 0)
    cost = imp_cost.reshape(4, BLOCK).astype(jnp.float32)
    blk4, plus, minus = shift_z(blk, 4), shift_z(blk, 2), shift_z(blk, -2)
    near = other_core(imp_emb)
    bar = lax.optimization_barrier
    blk4, emb, blk = bar((blk4, imp_emb, blk))
    pair = jnp.concatenate([blk, blk4], 0)
    up, down = shift_z(pair, 1), shift_z(pair, -1)
    b = jnp.concatenate([blk, blk4, plus, minus], 0)
    b_up, b_down = shift_y(b, 1), shift_y(b, -1)
    left, right, across = shift_x(emb, 1), shift_x(emb, -1), shift_x(emb, 2)
    a = jnp.concatenate([up, down], 0)
    a_up, a_down = shift_y(a, 1), shift_y(a, -1)
    b_down, left = bar((b_down, left))
    b_two = shift_y(b_down, -1)
    a_up, left, right, groups, cost = bar((a_up, left, right, groups, cost))
    a_two = shift_y(a_up, 1)
    oleft, oright = other_core(left), other_core(right)
    rows_in = [pltpu.with_memory_space_constraint(imp_emb, pltpu.HBM), left, right, across, near, oleft, oright, other_core(across)]
    camps = [a, b, a_up, a_down, b_up, b_down, a_two, b_two]

    stat, expo, tops = pl.pallas_call(
        stats_kernel,
        in_specs=[SM] * 2 + [pl.BlockSpec(memory_space=pl.ANY)] * 8 + [VM] * 9,
        out_specs=[VM] * 3,
        out_shape=[
            OUT((NX * NC, 2 * TILES + 8, BLOCK), jnp.float32),
            OUT((2 * GROUPS, BLOCK, BLOCK), jnp.float32),
            OUT((TRASH + 2, 8, BLOCK), jnp.float32),
        ],
        scratch_shapes=[
            pltpu.VMEM((TILES * BLOCK, D), jnp.bfloat16),
            pltpu.VMEM((OWN + 1, BLOCK, D), jnp.bfloat16),
            pltpu.VMEM((OWN + 1, BLOCK, BLOCK), jnp.float32),
            pltpu.VMEM((TRASH + 2, 8, BLOCK), jnp.float32),
            pltpu.SemaphoreType.DMA((8,)),
        ],
        compiler_params=params,
        name="stats",
    )(groups, where, *rows_in, *(pltpu.with_memory_space_constraint(v, pltpu.VMEM) for v in camps), cost)

    stats = lax.all_to_all(stat, "camp", 0, 0)

    spend, logz = pl.pallas_call(
        spend_kernel,
        in_specs=[SM] + [VM] * 3,
        out_specs=[VM] * 2,
        out_shape=[
            OUT((OWN, BLOCK), jnp.float32),
            jax.ShapeDtypeStruct((TILES, BLOCK), jnp.float32),
        ],
        scratch_shapes=[
            pltpu.VMEM((OWN + 1, BLOCK, BLOCK), jnp.float32),
            pltpu.VMEM((2 * TILES, BLOCK), jnp.float32),
        ],
        compiler_params=params,
        name="spend",
    )(groups, stats, expo, tops)

    mine = jnp.sum(lax.all_to_all(spend, "imp", 0, 0), axis=0)
    new_prices = prices.astype(jnp.float32) + 2.0 * (mine - spend_limits) / (mine + spend_limits)
    return (new_prices, logz.reshape(TILES * BLOCK))


def solution(mesh):
    return jax.shard_map(
        local,
        mesh=mesh,
        in_specs=(
            P(("imp", "camp"), None),
            P(("imp", "camp")),
            P(("camp", "imp"), None),
            P(("camp", "imp")),
            P(("camp", "imp")),
            P("imp", "camp", None),
            P("imp", "camp"),
        ),
        out_specs=(P(("camp", "imp")), P("imp")),
        check_vma=False,
    )
```
